512 devices in a mesh: row: 32 (over x, z), col: 16 (over y, core).
Axes of the slice: x: 4, y: 8, z: 8, core: 2. Of those that a mesh axis runs over, the one named last changes fastest.
Arguments:
- features: bfloat16 [1024, 512, 256], P('row', 'col'), may hold values from -6 to 6
- tower_weight: bfloat16 [2, 3, 3, 256, 256], replicated, may hold values from -0.1875 to 0.1875
- tower_bias: float32 [2, 256], replicated, may hold values from -3 to 3
- boxes: int32 [512, 4], P('row'), may hold values from 0 to 1023, as said below
- owner_slot: int32 [32, 16], P('row'), may hold values from 0 to 15, each once within a row
- mask_weight: bfloat16 [1, 3, 3, 256, 256], replicated, may hold values from -0.1875 to 0.1875
- mask_bias: float32 [1, 256], replicated, may hold values from -3 to 3
- deconv_weight: bfloat16 [2, 2, 256, 256], replicated, may hold values from -0.375 to 0.375
- deconv_bias: float32 [256], replicated, may hold values from -3 to 3
Outputs:
- tower: bfloat16 [1024, 512, 256], P('row', 'col')
- masks: bfloat16 [512, 28, 28, 256], P(('row', 'col'))
The draws below stay inside these ranges and needn't reach their ends.
Inputs may be any that keep to these rules, and one draw needn't show every extreme that they name: `boxes`: row k is (top, left, height, width) of region k in feature pixels: the box lies inside the image, height 1 to 32, width 1 to 64, and its top row is among rows 32 * g to 32 * g + 31 with g = k // 16. The first region of every group has height 32 and width 64. Region 0 has top 0 and left 0; the last region is the single pixel at the image's bottom right corner.
All inputs are finite; a program needn't handle non-finite values.
Results may differ from the reference program's by a relative error of at most 0.0066.
Values may be sent and summed in bfloat16 or wider, within the bound.
No kernel may reach another device: no remote copies, remote signals or barrier semaphores. Data moves between devices by JAX's collectives and lax.ppermute only.
A program may use at most 64 MiB of HBM per device.

```python
import jax
import jax.numpy as jnp
from jax import lax

C = 256
POOL = 14
TOWER = 2
MASK_LAYERS = 1
BOXW = 64
RH = 32
H = 1024
W = 512
REG_ROW = 16
REGIONS = 512
N_ROW = 32


def draw_boxes(key, part):
    key = jax.random.fold_in(key, 11)
    key_height, key_width, key_top, key_left = jax.random.split(key, 4)
    indices = jnp.arange(REGIONS, dtype=jnp.int32)
    slot_index = indices % REG_ROW
    group_index = indices // REG_ROW
    last_region = indices == REGIONS - 1
    first_region = indices == 0
    heights = jax.random.randint(key_height, (REGIONS,), 1, RH + 1)
    heights = jnp.where(slot_index == 0, RH, heights)
    heights = jnp.where(last_region, 1, heights)
    widths = jax.random.randint(key_width, (REGIONS,), 1, BOXW + 1)
    widths = jnp.where(slot_index == 0, BOXW, widths)
    widths = jnp.where(last_region, 1, widths)
    top_lower = group_index * RH
    room = jnp.minimum(RH, H - heights - top_lower + 1)
    tops = top_lower + jax.random.randint(key_top, (REGIONS,), 0, room)
    tops = jnp.where(last_region, H - 1, tops)
    tops = jnp.where(first_region, 0, tops)
    lefts = jax.random.randint(key_left, (REGIONS,), 0, W - widths + 1)
    lefts = jnp.where(last_region, W - 1, lefts)
    lefts = jnp.where(first_region, 0, lefts)
    return jnp.stack([tops, lefts, heights, widths], axis=1).astype(jnp.int32)


def steps_of(key, dims, shards, least, largest):
    def one(dim, blocks):
        steps = jax.random.uniform(jax.random.fold_in(jax.random.fold_in(key, 6), dim), (blocks,), jnp.float32, least / len(shards), largest / len(shards))
        return jnp.repeat(jnp.exp(steps), dims[dim] // blocks).reshape((-1,) + (1,) * (len(dims) - dim - 1))

    level = one(*shards[0])
    for cut in shards[1:]:
        level = level * one(*cut)
    return level


def noise(stream_key, dims, deviation, most, pieces=(), held_as=jnp.bfloat16):
    entries = jax.random.normal(stream_key, dims, jnp.float32) * deviation
    if len(pieces) > 0:
        entries = steps_of(stream_key, dims, pieces, -0.22, 0.18) * entries
    return jnp.clip(entries, min=-most, max=most).astype(held_as)


def setup_inputs(seed: int = 0) -> dict:
    splits = jax.random.split(jax.random.key(seed), 10)
    return {
        "features": noise(splits[0], (H, W, C), 1.0, 6.0, ((0, 32), (1, 16))),
        "tower_weight": noise(splits[1], (TOWER, 3, 3, C, C), (4 * C) ** -0.5, 0.1875),
        "tower_bias": noise(splits[2], (TOWER, C), 0.5, 3.0, (), jnp.float32),
        "boxes": draw_boxes(jax.random.fold_in(splits[9], 71), 0),
        "owner_slot": jax.vmap(lambda own: jax.random.permutation(own, REG_ROW))(jax.random.split(splits[4], N_ROW)).reshape((N_ROW, REG_ROW)).astype(jnp.int32),
        "mask_weight": noise(splits[5], (MASK_LAYERS, 3, 3, C, C), (4 * C) ** -0.5, 0.1875),
        "mask_bias": noise(splits[6], (MASK_LAYERS, C), 0.5, 3.0, (), jnp.float32),
        "deconv_weight": noise(splits[7], (2, 2, C, C), C ** -0.5, 0.375),
        "deconv_bias": noise(splits[8], (C,), 0.5, 3.0, (), jnp.float32),
    }


def convolve(padded, kernel, bias_row):
    rows_out = padded.shape[-3] - 2
    cols_out = padded.shape[-2] - 2
    leading = padded.shape[:-3]
    channels = kernel.shape[-1]
    running = None
    for row_step in range(3):
        for col_step in range(3):
            window = padded[..., row_step:row_step + rows_out, col_step:col_step + cols_out, :]
            window = window.reshape(-1, padded.shape[-1])
            product = jnp.dot(window, kernel[row_step, col_step], preferred_element_type=jnp.float32)
            running = product if running is None else running + product
    running = jnp.maximum(running + bias_row, 0.0)
    return running.reshape(leading + (rows_out, cols_out, channels)).astype(jnp.bfloat16)


def bilinear_ramp(lower, extent, coords):
    lower_f = lower.astype(jnp.float32)[:, None, None]
    extent_f = extent.astype(jnp.float32)[:, None, None]
    bins = jnp.arange(POOL).astype(jnp.float32)[None, :, None]
    centre = lower_f + (bins + 0.5) * extent_f / POOL - 0.5
    centre = jnp.clip(centre, lower_f, lower_f + extent_f - 1.0)
    places = coords.astype(jnp.float32)[None, None, :]
    return jnp.maximum(1.0 - jnp.abs(places - centre), 0.0).astype(jnp.bfloat16)


def mask_head(pooled, mask_weight, mask_bias, deconv_weight, deconv_bias):
    hidden = pooled
    for layer_index in range(mask_weight.shape[0]):
        padded = jnp.pad(hidden, ((0, 0), (1, 1), (1, 1), (0, 0)))
        hidden = convolve(padded, mask_weight[layer_index], mask_bias[layer_index])
    lifted = jnp.einsum("rabc,uvcd->raubvd", hidden.astype(jnp.float32), deconv_weight.astype(jnp.float32))
    lifted = jnp.maximum(lifted + deconv_bias, 0.0)
    return lifted.reshape(hidden.shape[0], 2 * POOL, 2 * POOL, -1).astype(jnp.bfloat16)


def reference(features, tower_weight, tower_bias, boxes, owner_slot, mask_weight, mask_bias, deconv_weight, deconv_bias):
    tower = features
    for layer_index in range(TOWER):
        padded = jnp.pad(tower, ((1, 1), (1, 1), (0, 0)))
        tower = convolve(padded, tower_weight[layer_index], tower_bias[layer_index])
    groups = REGIONS // REG_ROW
    inverse = jnp.argsort(owner_slot, axis=1).astype(jnp.int32)
    order = (jnp.arange(groups, dtype=jnp.int32)[:, None] * REG_ROW + inverse).reshape(-1)
    ordered = boxes[order]

    def pool_one(box):
        row_anchor = jnp.minimum(box[0], H - RH).astype(jnp.int32)
        col_anchor = jnp.minimum(box[1], W - BOXW).astype(jnp.int32)
        window = lax.dynamic_slice(tower, (row_anchor, col_anchor, jnp.zeros((), jnp.int32)), (RH, BOXW, C))
        down = bilinear_ramp(box[0:1], box[2:3], row_anchor + jnp.arange(RH, dtype=jnp.int32))[0]
        across = bilinear_ramp(box[1:2], box[3:4], col_anchor + jnp.arange(BOXW, dtype=jnp.int32))[0]
        partial_sum = jnp.einsum("qx,yxc->yqc", across.astype(jnp.float32), window.astype(jnp.float32), precision=lax.Precision.HIGHEST)
        return jnp.einsum("py,yqc->pqc", down.astype(jnp.float32), partial_sum, precision=lax.Precision.HIGHEST)

    pooled = lax.map(pool_one, ordered).astype(jnp.bfloat16)
    blocks = pooled.reshape(groups, REG_ROW, POOL, POOL, C)

    def head_block(block):
        return mask_head(block, mask_weight, mask_bias, deconv_weight, deconv_bias)

    masks = lax.map(head_block, blocks)
    return tower, masks.reshape(REGIONS, 2 * POOL, 2 * POOL, C)
```

```python
import jax
import jax.numpy as jnp
from jax import lax
from jax.experimental import pallas as pl
from jax.experimental.pallas import tpu as pltpu
from jax.sharding import PartitionSpec as P

POOL = 14
SIDE = 16
LANES = 128
FIRST = 11
SECOND = 8
F32 = jnp.float32
BF16 = jnp.bfloat16


def shift(value, axis, step):
    devices = range(lax.axis_size(axis))
    return lax.ppermute(value, axis, [(i, i + step) for i in devices if i + step in devices])


def conv_valid(padded, kernel, bias):
    out = lax.conv_general_dilated(
        padded[None], kernel, (1, 1), "VALID",
        dimension_numbers=("NHWC", "HWIO", "NHWC"), preferred_element_type=F32,
    )[0]
    return jnp.maximum(out + bias, 0.0).astype(BF16)


def exchange(features, weight, bias):
    rows, cols, channels = features.shape
    row, col = lax.axis_index("row"), lax.axis_index("col")
    last_row, last_col = lax.axis_size("row") - 1, lax.axis_size("col") - 1
    below = shift(features, "row", -1)
    left = shift(features[:, cols - 2 :], "col", 1)
    right = shift(features[:, :2], "col", -1)
    own = jnp.concatenate([left, features, right], axis=1)
    own_sides = jnp.concatenate([left, features[:, :1], features[:, cols - 1 :], right], axis=1)
    sides = shift(own_sides, "row", -1)
    above = shift(own[rows - 2 :], "row", 1)
    after = shift(own[:1], "row", -2)

    def ends(strip):
        return jnp.concatenate([strip[:, :3], strip[:, cols + 1 :]], axis=1)

    columns = jnp.concatenate([ends(above), own_sides, sides, ends(after)], axis=0)
    edge = jnp.pad(columns[:, 1:5:3].astype(F32), ((0, 1), (0, 0), (0, 0)))
    edge = edge.swapaxes(0, 1)[:, :, None]
    batch = columns.reshape(-1, 2, 3, channels).swapaxes(0, 1)
    inner = lax.conv_general_dilated(
        batch, weight[0], (1, 1), "VALID",
        dimension_numbers=("NHWC", "HWIO", "NHWC"), preferred_element_type=F32,
    )
    inner = jnp.maximum(inner + bias[0], 0.0).astype(BF16).astype(F32)
    kept = jnp.stack([col > 0, col < last_col])[:, None, None, None]
    inner = jnp.pad(jnp.where(kept, inner, 0.0), ((0, 0), (0, 1), (0, 0), (0, 0)))
    flags = jnp.stack([row == 0, row == last_row]).astype(jnp.int32)
    return below, above[:, 2 : cols + 2], after[:, 2 : cols + 2], edge, inner, flags


def sample(lower, extent):
    lower_f = lower.astype(F32)[:, None]
    extent_f = extent.astype(F32)[:, None]
    bins = jnp.arange(POOL).astype(F32)[None, :]
    centre = lower_f + (bins + 0.5) * extent_f / POOL - 0.5
    return jnp.clip(centre, lower_f, lower_f + extent_f - 1.0)


def spread(dst, start, value, edges, offset):
    count, width, channels = value.shape
    value = value.astype(F32)
    place = lax.broadcasted_iota(jnp.int32, value.shape, 1)
    here = pl.ds(offset, count)
    before = jnp.where(place == 0, edges[0, here], pltpu.roll(value, 1, 1))
    after = jnp.where(place == width - 1, edges[1, here], pltpu.roll(value, width - 1, 1))
    rows = pl.ds(start, count)
    dst[rows, :, 0:channels] = before.astype(BF16)
    dst[rows, :, channels : 2 * channels] = value.astype(BF16)
    dst[rows, :, 2 * channels : 3 * channels] = after.astype(BF16)


def taps(src, start, count, weight, bias):
    width, depth = src.shape[1:]
    parts = [src[pl.ds(start + d, count)].reshape(count * width, depth) for d in range(3)]
    out = jnp.dot(jnp.concatenate(parts, axis=1), weight, preferred_element_type=F32)
    out = jnp.maximum(out + bias, 0.0)
    return out.reshape(count, width, out.shape[-1])


def main_kernel(
    flags_ref, hit_ref, xa_ref, xb_ref, wa_ref, wb_ref,
    own_ref, below_ref, above_ref, after_ref, edge_ref, inner_ref,
    weight_ref, bias_ref, down_ref,
    tower_ref, mine_ref, other_ref,
    wide_ref, mid_ref, band_ref, pooled_ref, patch_ref,
):
    rows, width, channels = own_ref.shape
    half = mine_ref.shape[0]
    spread(wide_ref, 0, above_ref[...], edge_ref, 0)
    step = 8
    for part, base in ((own_ref, 2), (below_ref, 2 + rows)):
        def fill(i, carry):
            at = i * step
            spread(wide_ref, base + at, part[pl.ds(at, step)], edge_ref, base + at)
            return carry

        lax.fori_loop(0, rows // step, fill, 0)
    spread(wide_ref, 2 + 2 * rows, after_ref[...], edge_ref, 2 + 2 * rows)
    wide_ref[3 + 2 * rows] = jnp.zeros(wide_ref.shape[1:], BF16)

    def first(i, carry):
        at = i * FIRST
        out = taps(wide_ref, at, FIRST, weight_ref[0], bias_ref[0:1])
        spread(mid_ref, at, out.astype(BF16), inner_ref, at)
        return carry

    lax.fori_loop(0, (2 * rows + 2) // FIRST, first, 0)
    blank = jnp.zeros(mid_ref.shape[1:], BF16)

    @pl.when(flags_ref[0] > 0)
    def _():
        mid_ref[0] = blank

    @pl.when(flags_ref[1] > 0)
    def _():
        mid_ref[rows + 1] = blank
    mid_ref[2 * rows + 1] = blank

    def second(i, carry):
        at = i * SECOND
        out = taps(mid_ref, at, SECOND, weight_ref[1], bias_ref[1:2])

        @pl.when(at < rows)
        def _():
            tower_ref[pl.ds(at, SECOND)] = out.astype(BF16)

        for k in range(SECOND):
            line = out[k].astype(BF16).astype(F32)
            for h in range(channels // LANES):
                piece = line[:, h * LANES : (h + 1) * LANES]
                band_ref[h, pl.ds(at + k, width, stride=2 * rows), :] = piece
        return carry

    lax.fori_loop(0, 2 * rows // SECOND, second, 0)
    down = down_ref[...]

    def contract(x, carry):
        here = pl.ds(pl.multiple_of(x * 2 * rows, 2 * rows), 2 * rows)
        rhs = jnp.concatenate([band_ref[h, here, :] for h in range(channels // LANES)], axis=1)
        rhs = rhs.astype(BF16)
        pooled_ref[x] = jnp.dot(down, rhs, preferred_element_type=F32)
        return carry

    lax.fori_loop(0, width, contract, 0, unroll=4)
    for side, out_ref in ((1, other_ref), (0, mine_ref)):
        def region(m, carry):
            n = m + side * half
            base = pl.multiple_of(n * SIDE, SIDE)

            @pl.when(hit_ref[n] > 0)
            def _():
                for q in range(POOL):
                    one = pooled_ref[xa_ref[n, q], pl.ds(base, SIDE), :] * wa_ref[n, q]
                    two = pooled_ref[xb_ref[n, q], pl.ds(base, SIDE), :] * wb_ref[n, q]
                    total = one + two
                    for h in range(channels // LANES):
                        piece = total[:, h * LANES : (h + 1) * LANES]
                        patch_ref[h, pl.ds(q, SIDE, stride=SIDE), :] = piece
                for h in range(channels // LANES):
                    piece = patch_ref[h, pl.ds(0, POOL * SIDE), :]
                    out_ref[m, :, h * LANES : (h + 1) * LANES] = piece.astype(BF16)

            @pl.when(hit_ref[n] == 0)
            def _():
                out_ref[m] = jnp.zeros(out_ref.shape[1:], BF16)

            return carry

        lax.fori_loop(0, half, region, 0)


def weights_of(boxes, rows, cols):
    count = boxes.shape[0]
    row_first = lax.axis_index("row") * rows
    col_first = lax.axis_index("col") * cols
    places = (row_first + jnp.arange(2 * rows)).astype(F32)[None, None, :]
    centre = sample(boxes[:, 0], boxes[:, 2])
    down = jnp.maximum(1.0 - jnp.abs(places - centre[:, :, None]), 0.0).astype(BF16)
    down = jnp.pad(down, ((0, 0), (0, SIDE - POOL), (0, 0))).reshape(count * SIDE, 2 * rows)
    centre = sample(boxes[:, 1], boxes[:, 3])
    low = jnp.floor(centre)

    def tap(place):
        weight = jnp.maximum(1.0 - jnp.abs(place - centre), 0.0).astype(BF16).astype(F32)
        at = place.astype(jnp.int32) - col_first
        inside = (at >= 0) & (at < cols)
        return jnp.clip(at, 0, cols - 1), jnp.where(inside, weight, 0.0)

    xa, wa = tap(low)
    xb, wb = tap(low + 1.0)
    hit = (boxes[:, 1] < col_first + cols) & (boxes[:, 1] + boxes[:, 3] > col_first)
    return hit.astype(jnp.int32), xa, xb, wa, wb, down


def tower_and_pool(features, weight, bias, boxes):
    rows, cols, channels = features.shape
    below, above, after, edge, inner, flags = exchange(features, weight, bias)
    hit, xa, xb, wa, wb, down = weights_of(boxes, rows, cols)
    count = boxes.shape[0]
    smem = pl.BlockSpec(memory_space=pltpu.SMEM)
    vmem = pl.BlockSpec(memory_space=pltpu.VMEM)
    patches = jax.ShapeDtypeStruct((count // 2, POOL * SIDE, channels), BF16)
    return pl.pallas_call(
        main_kernel,
        out_shape=(jax.ShapeDtypeStruct(features.shape, BF16), patches, patches),
        in_specs=[smem] * 6 + [vmem] * 9,
        out_specs=(vmem, vmem, vmem),
        scratch_shapes=[
            pltpu.VMEM((2 * rows + 4, cols, 3 * channels), BF16),
            pltpu.VMEM((2 * rows + 2, cols, 3 * channels), BF16),
            pltpu.VMEM((channels // LANES, 2 * rows * cols, LANES), F32),
            pltpu.VMEM((cols, count * SIDE, channels), F32),
            pltpu.VMEM((channels // LANES, SIDE * SIDE, LANES), F32),
        ],
        compiler_params=pltpu.CompilerParams(vmem_limit_bytes=40 * 2**20),
        cost_estimate=pl.CostEstimate(flops=6 * 10**9, bytes_accessed=8 * 10**6, transcendentals=0),
    )(
        flags, hit, xa, xb, wa, wb, features, below, above, after, edge, inner,
        weight.reshape(2, 9 * channels, channels), bias, down,
    )


def head(pooled, mask_weight, mask_bias, deconv_weight, deconv_bias):
    padded = jnp.pad(pooled, ((1, 1), (1, 1), (0, 0)))
    hidden = conv_valid(padded, mask_weight[0], mask_bias[0])
    lifted = jnp.einsum("abc,uvcd->aubvd", hidden, deconv_weight, preferred_element_type=F32)
    lifted = jnp.maximum(lifted + deconv_bias, 0.0).astype(BF16)
    return lifted.reshape(1, 2 * POOL, 2 * POOL, -1)


def per_device(
    features, tower_weight, tower_bias, boxes, owner_slot,
    mask_weight, mask_bias, deconv_weight, deconv_bias,
):
    peers = lax.axis_size("col")
    chips = peers // 2
    core = lax.axis_index("col") % 2
    slots = jnp.arange(peers, dtype=jnp.int32)
    wanted = 2 * (slots % chips) + jnp.where(slots < chips, core, 1 - core)
    picked = (owner_slot[0][None, :] == wanted[:, None]).astype(jnp.int32)
    ordered = jnp.sum(picked[:, :, None] * boxes[None, :, :], axis=1)
    tower, mine, other = tower_and_pool(features, tower_weight, tower_bias, ordered)
    swapped = lax.ppermute(other, "col", [(i, i ^ 1) for i in range(peers)])
    chip_sum = (mine.astype(F32) + swapped.astype(F32)).astype(BF16)
    groups = [list(range(0, peers, 2)), list(range(1, peers, 2))]
    parts = lax.all_to_all(chip_sum, "col", 0, 0, tiled=True, axis_index_groups=groups)
    pooled = jnp.sum(parts.astype(F32), axis=0).astype(BF16)
    pooled = pooled.reshape(POOL, SIDE, -1)[:, :POOL]
    masks = head(pooled, mask_weight, mask_bias, deconv_weight, deconv_bias)
    return tower, masks


def solution(mesh):
    placed = (P("row", "col", None), P(), P(), P("row", None), P("row", None), P(), P(), P(), P())
    return jax.shard_map(
        per_device,
        mesh=mesh,
        in_specs=placed,
        out_specs=(P("row", "col", None), P(("row", "col"), None, None, None)),
        check_vma=False,
    )
```

```python
import jax
import jax.numpy as jnp
from jax import lax
from jax.experimental import pallas as pl
from jax.experimental.pallas import tpu as pltpu
from jax.sharding import PartitionSpec as P

POOL = 14
SIDE = 16
LANES = 128
TILE = 16
FIRST = 11
SECOND = 8
HOPS = (4, 1, -1, 2, -3, 3, -2, 0)
F32 = jnp.float32
BF16 = jnp.bfloat16


def shift(value, axis, step):
    devices = range(lax.axis_size(axis))
    return lax.ppermute(value, axis, [(i, i + step) for i in devices if i + step in devices])


def conv_valid(padded, kernel, bias):
    out = lax.conv_general_dilated(
        padded[None], kernel, (1, 1), "VALID",
        dimension_numbers=("NHWC", "HWIO", "NHWC"), preferred_element_type=F32,
    )[0]
    return jnp.maximum(out + bias, 0.0).astype(BF16)


def call(kernel, out_shape, in_specs, scratch, limit, flops, *args):
    vmem = pl.BlockSpec(memory_space=pltpu.VMEM)
    return pl.pallas_call(
        kernel,
        out_shape=out_shape,
        in_specs=in_specs,
        out_specs=tuple(vmem for _ in out_shape),
        scratch_shapes=scratch,
        compiler_params=pltpu.CompilerParams(vmem_limit_bytes=limit * 2**20),
        cost_estimate=pl.CostEstimate(flops=flops, bytes_accessed=10**6, transcendentals=0),
    )(*args)


def columns_kernel(tile_ref, lead_ref, tail_ref, flat_ref):
    rows, width, channels = tile_ref.shape
    for out_ref, first, start in ((lead_ref, 0, 0), (tail_ref, TILE - 2, width - TILE)):
        block = tile_ref[:, pl.ds(start, TILE), :].astype(F32).reshape(rows * TILE, channels)
        for h in range(channels // LANES):
            flat_ref[h] = block[:, h * LANES : (h + 1) * LANES]
        for x in range(2):
            here = pl.ds(first + x, rows, stride=TILE)
            column = [flat_ref[h, here, :] for h in range(channels // LANES)]
            out_ref[x] = jnp.concatenate(column, axis=1).astype(BF16)


def pack_kernel(tile_ref, left_ref, right_ref, lead_ref, tail_ref, sides_ref, down_ref, up_ref):
    rows, width, channels = tile_ref.shape
    parts = (left_ref[0], left_ref[1], lead_ref[0], tail_ref[1], right_ref[0], right_ref[1])
    whole = width // TILE
    down_ref[0 : 2 * whole] = tile_ref[rows - 2 : rows].reshape(2 * whole, TILE, channels)
    up_ref[0:whole] = tile_ref[0:1].reshape(whole, TILE, channels)
    for i, part in enumerate(parts):
        sides_ref[i] = part
        down_ref[2 * whole + i] = part[rows - TILE : rows]
        up_ref[whole + i] = part[0:TILE]


def exchange(features, later):
    rows, cols, channels = features.shape
    vmem = pl.BlockSpec(memory_space=pltpu.VMEM)
    below = shift(features, "row", -1)
    pair = jax.ShapeDtypeStruct((2, rows, channels), BF16)
    lead, tail = call(
        columns_kernel, (pair, pair), [vmem],
        [pltpu.VMEM((channels // LANES, rows * TILE, LANES), F32)], 4, 10**5, features,
    )
    left = shift(tail, "col", 1)
    right = shift(lead, "col", -1)
    whole = cols // TILE
    shapes = [(6, rows), (2 * whole + 6, TILE), (whole + 6, TILE)]
    own_sides, to_down, to_up = call(
        pack_kernel,
        tuple(jax.ShapeDtypeStruct(shape + (channels,), BF16) for shape in shapes),
        [vmem] * 5, [], 4, 10**5, features, left, right, lead, tail,
    )
    sides = shift(own_sides, "row", -1)
    after, later = lax.optimization_barrier((shift(to_up, "row", -2), later))
    above = shift(to_down, "row", 1)
    return below, own_sides, sides, above, after, later


def sample(lower, extent):
    lower_f = lower.astype(F32)[:, None]
    extent_f = extent.astype(F32)[:, None]
    bins = jnp.arange(POOL).astype(F32)[None, :]
    centre = lower_f + (bins + 0.5) * extent_f / POOL - 0.5
    return jnp.clip(centre, lower_f, lower_f + extent_f - 1.0)


def spread(dst, start, value, edge_ref, sides, offset):
    count, width, channels = value.shape
    place = lax.broadcasted_iota(jnp.int32, (width, channels), 0)
    for k in range(count):
        line = value[k].astype(F32)
        low = edge_ref[sides[0], pl.ds(offset + k, 1), :]
        high = edge_ref[sides[1], pl.ds(offset + k, 1), :]
        before = jnp.where(place == 0, low, pltpu.roll(line, 1, 0))
        after = jnp.where(place == width - 1, high, pltpu.roll(line, width - 1, 0))
        dst[start + k, :, 0:channels] = before.astype(BF16)
        dst[start + k, :, channels : 2 * channels] = line.astype(BF16)
        dst[start + k, :, 2 * channels : 3 * channels] = after.astype(BF16)


def taps(src, start, count, weight, bias):
    width, depth = src.shape[1:]
    parts = [src[pl.ds(start + d, count)].reshape(count * width, depth) for d in range(3)]
    out = jnp.dot(jnp.concatenate(parts, axis=1), weight, preferred_element_type=F32)
    out = jnp.maximum(out + bias, 0.0)
    return out.reshape(count, width, out.shape[-1])


def main_kernel(
    flags_ref, hit_ref, xa_ref, xb_ref, wa_ref, wb_ref,
    own_ref, below_ref, own_sides_ref, sides_ref, above_ref, after_ref,
    weight_ref, bias_ref, down_ref,
    tower_ref, mine_ref, other_ref,
    wide_ref, mid_ref, band_ref, pooled_ref, patch_ref, strip_ref, inner_ref,
):
    rows, width, channels = own_ref.shape
    half = mine_ref.shape[0]
    whole = width // TILE
    for c in range(6):
        strip_ref[c, 0:2, :] = above_ref[2 * whole + c].astype(F32)[TILE - 2 : TILE]
        strip_ref[c, 2 : rows + 2, :] = own_sides_ref[c].astype(F32)
        strip_ref[c, rows + 2 : 2 * rows + 2, :] = sides_ref[c].astype(F32)
        strip_ref[c, 2 * rows + 2 : 2 * rows + 3, :] = after_ref[whole + c].astype(F32)[0:1]
        tail = strip_ref.shape[1] - (2 * rows + 3)
        strip_ref[c, 2 * rows + 3 :, :] = jnp.zeros((tail, channels), F32)
    for side in range(2):
        tall = inner_ref.shape[1]
        parts = [
            strip_ref[3 * side + dx, dy : dy + tall, :].astype(BF16)
            for dy in range(3)
            for dx in range(3)
        ]
        out = jnp.dot(
            jnp.concatenate(parts, axis=1), weight_ref[0], preferred_element_type=F32
        )
        out = jnp.maximum(out + bias_ref[0:1], 0.0).astype(BF16).astype(F32)
        inner_ref[side] = jnp.where(flags_ref[2 + side] > 0, out, 0.0)
    spread(wide_ref, 0, above_ref[0 : 2 * whole].reshape(2, width, channels), strip_ref, (1, 4), 0)
    step = 8
    for part, base in ((own_ref, 2), (below_ref, 2 + rows)):
        def fill(i, carry):
            at = i * step
            spread(wide_ref, base + at, part[pl.ds(at, step)], strip_ref, (1, 4), base + at)
            return carry

        lax.fori_loop(0, rows // step, fill, 0)
    last = 2 + 2 * rows
    spread(wide_ref, last, after_ref[0:whole].reshape(1, width, channels), strip_ref, (1, 4), last)
    wide_ref[3 + 2 * rows] = jnp.zeros(wide_ref.shape[1:], BF16)

    def first(i, carry):
        at = i * FIRST
        out = taps(wide_ref, at, FIRST, weight_ref[0], bias_ref[0:1])
        spread(mid_ref, at, out.astype(BF16), inner_ref, (0, 1), at)
        return carry

    lax.fori_loop(0, (2 * rows + 2) // FIRST, first, 0)
    blank = jnp.zeros(mid_ref.shape[1:], BF16)

    @pl.when(flags_ref[0] > 0)
    def _():
        mid_ref[0] = blank

    @pl.when(flags_ref[1] > 0)
    def _():
        mid_ref[rows + 1] = blank
    mid_ref[2 * rows + 1] = blank

    def second(i, carry):
        at = i * SECOND
        out = taps(mid_ref, at, SECOND, weight_ref[1], bias_ref[1:2])

        @pl.when(at < rows)
        def _():
            tower_ref[pl.ds(at, SECOND)] = out.astype(BF16)

        for k in range(SECOND):
            line = out[k].astype(BF16).astype(F32)
            for h in range(channels // LANES):
                piece = line[:, h * LANES : (h + 1) * LANES]
                band_ref[h, pl.ds(at + k, width, stride=2 * rows), :] = piece
        return carry

    lax.fori_loop(0, 2 * rows // SECOND, second, 0)
    down = down_ref[...]

    def contract(x, carry):
        here = pl.ds(pl.multiple_of(x * 2 * rows, 2 * rows), 2 * rows)
        rhs = jnp.concatenate([band_ref[h, here, :] for h in range(channels // LANES)], axis=1)
        rhs = rhs.astype(BF16)
        pooled_ref[x] = jnp.dot(down, rhs, preferred_element_type=F32)
        return carry

    lax.fori_loop(0, width, contract, 0, unroll=4)
    for side, out_ref in ((1, other_ref), (0, mine_ref)):
        def region(m, carry):
            n = m + side * half
            base = pl.multiple_of(n * SIDE, SIDE)

            @pl.when(hit_ref[n] > 0)
            def _():
                for q in range(POOL):
                    one = pooled_ref[xa_ref[n, q], pl.ds(base, SIDE), :] * wa_ref[n, q]
                    two = pooled_ref[xb_ref[n, q], pl.ds(base, SIDE), :] * wb_ref[n, q]
                    total = one + two
                    for h in range(channels // LANES):
                        piece = total[:, h * LANES : (h + 1) * LANES]
                        patch_ref[h, pl.ds(q, SIDE, stride=POOL), :] = piece
                for h in range(channels // LANES):
                    piece = patch_ref[h, pl.ds(0, POOL * POOL), :]
                    out_ref[m, :, h * LANES : (h + 1) * LANES] = piece.astype(BF16)

            @pl.when(hit_ref[n] == 0)
            def _():
                out_ref[m] = jnp.zeros(out_ref.shape[1:], BF16)

            return carry

        lax.fori_loop(0, half, region, 0)


def weights_of(boxes, rows, cols):
    count = boxes.shape[0]
    row_first = lax.axis_index("row") * rows
    col_first = lax.axis_index("col") * cols
    places = (row_first + jnp.arange(2 * rows)).astype(F32)[None, None, :]
    centre = sample(boxes[:, 0], boxes[:, 2])
    down = jnp.maximum(1.0 - jnp.abs(places - centre[:, :, None]), 0.0).astype(BF16)
    down = jnp.pad(down, ((0, 0), (0, SIDE - POOL), (0, 0))).reshape(count * SIDE, 2 * rows)
    centre = sample(boxes[:, 1], boxes[:, 3])
    low = jnp.floor(centre)

    def tap(place):
        weight = jnp.maximum(1.0 - jnp.abs(place - centre), 0.0).astype(BF16).astype(F32)
        at = place.astype(jnp.int32) - col_first
        inside = (at >= 0) & (at < cols)
        return jnp.clip(at, 0, cols - 1), jnp.where(inside, weight, 0.0)

    xa, wa = tap(low)
    xb, wb = tap(low + 1.0)
    hit = (boxes[:, 1] < col_first + cols) & (boxes[:, 1] + boxes[:, 3] > col_first)
    return hit.astype(jnp.int32), xa, xb, wa, wb, down


def tower_and_pool(features, weight, bias, boxes, owner_slot, wanted):
    rows, cols, channels = features.shape
    below, own_sides, sides, above, after, (boxes, owner_slot, wanted) = exchange(
        features, (boxes, owner_slot, wanted)
    )
    row, col = lax.axis_index("row"), lax.axis_index("col")
    last_row, last_col = lax.axis_size("row") - 1, lax.axis_size("col") - 1
    flags = jnp.stack([row == 0, row == last_row, col > 0, col < last_col]).astype(jnp.int32)
    picked = (owner_slot[0][None, :] == wanted[:, None]).astype(jnp.int32)
    boxes = jnp.sum(picked[:, :, None] * boxes[None, :, :], axis=1)
    hit, xa, xb, wa, wb, down = weights_of(boxes, rows, cols)
    count = boxes.shape[0]
    smem = pl.BlockSpec(memory_space=pltpu.SMEM)
    vmem = pl.BlockSpec(memory_space=pltpu.VMEM)
    patches = jax.ShapeDtypeStruct((count // 2, POOL * POOL, channels), BF16)
    return call(
        main_kernel,
        (jax.ShapeDtypeStruct(features.shape, BF16), patches, patches),
        [smem] * 6 + [vmem] * 9,
        [
            pltpu.VMEM((2 * rows + 4, cols, 3 * channels), BF16),
            pltpu.VMEM((2 * rows + 2, cols, 3 * channels), BF16),
            pltpu.VMEM((channels // LANES, 2 * rows * cols, LANES), F32),
            pltpu.VMEM((cols, count * SIDE, channels), F32),
            pltpu.VMEM((channels // LANES, SIDE * SIDE, LANES), F32),
            pltpu.VMEM((6, 2 * rows + 24, channels), F32),
            pltpu.VMEM((2, 2 * rows + 16, channels), F32),
        ],
        40, 6 * 10**9,
        flags, hit, xa, xb, wa, wb, features, below, own_sides, sides, above, after,
        weight.reshape(2, 9 * channels, channels), bias, down,
    )


def head(pooled, mask_weight, mask_bias, deconv_weight, deconv_bias):
    padded = jnp.pad(pooled, ((1, 1), (1, 1), (0, 0)))
    hidden = conv_valid(padded, mask_weight[0], mask_bias[0])
    lifted = jnp.einsum("abc,uvcd->aubvd", hidden, deconv_weight, preferred_element_type=F32)
    lifted = jnp.maximum(lifted + deconv_bias, 0.0).astype(BF16)
    return lifted.reshape(1, 2 * POOL, 2 * POOL, -1)


def per_device(
    features, tower_weight, tower_bias, boxes, owner_slot,
    mask_weight, mask_bias, deconv_weight, deconv_bias,
):
    peers = lax.axis_size("col")
    chips = peers // 2
    core = lax.axis_index("col") % 2
    chip = lax.axis_index("col") // 2
    hops = jnp.array(HOPS * 2, dtype=jnp.int32)
    sides = jnp.repeat(jnp.stack([core, 1 - core]), chips)
    wanted = 2 * ((chip + hops * (1 - 2 * sides)) % chips) + sides
    tower, mine, other = tower_and_pool(
        features, tower_weight, tower_bias, boxes, owner_slot, wanted
    )
    swapped = lax.ppermute(other, "col", [(i, i ^ 1) for i in range(peers)])

    def send(value, hop):
        steps = [2 * hop * (1 - 2 * (i % 2)) for i in range(peers)]
        return lax.ppermute(value, "col", [(i, (i + steps[i]) % peers) for i in range(peers)])

    def total(*parts):
        parts = [part.astype(F32) for part in parts]
        return sum(parts[1:], parts[0]).astype(BF16)

    ahead = send(total(mine[0:3], swapped[0:3]), 1)
    back = send(total(mine[3:5], swapped[3:5]), -1)
    three = send(total(mine[5], swapped[5], ahead[0], back[0]), 3)
    two = send(total(mine[6], swapped[6], ahead[2], back[1]), -2)
    pooled = total(mine[7], swapped[7], ahead[1], three, two)
    pooled = pooled.reshape(POOL, POOL, -1)
    masks = head(pooled, mask_weight, mask_bias, deconv_weight, deconv_bias)
    return tower, masks


def solution(mesh):
    placed = (P("row", "col", None), P(), P(), P("row", None), P("row", None), P(), P(), P(), P())
    return jax.shard_map(
        per_device,
        mesh=mesh,
        in_specs=placed,
        out_specs=(P("row", "col", None), P(("row", "col"), None, None, None)),
        check_vma=False,
    )
```

```python
import jax
import jax.numpy as jnp
from jax import lax
from jax.experimental import pallas as pl
from jax.experimental.pallas import tpu as pltpu
from jax.sharding import PartitionSpec as P

POOL = 14
SIDE = 16
LANES = 128
TILE = 16
FIRST = 33
SECOND = 32
HOPS = (4, 1, -1, 2, -3, 3, -2, 0)
F32 = jnp.float32
BF16 = jnp.bfloat16


def shift(value, axis, step):
    devices = range(lax.axis_size(axis))
    return lax.ppermute(value, axis, [(i, i + step) for i in devices if i + step in devices])


def call(kernel, out_shape, in_specs, scratch, limit, flops, *args):
    vmem = pl.BlockSpec(memory_space=pltpu.VMEM)
    return pl.pallas_call(
        kernel,
        out_shape=out_shape,
        in_specs=in_specs,
        out_specs=tuple(vmem for _ in out_shape),
        scratch_shapes=scratch,
        compiler_params=pltpu.CompilerParams(vmem_limit_bytes=limit * 2**20),
        cost_estimate=pl.CostEstimate(flops=flops, bytes_accessed=10**6, transcendentals=0),
    )(*args)


def columns_kernel(tile_ref, lead_ref, tail_ref, rim_ref, flat_ref):
    rows, width, channels = tile_ref.shape
    for out_ref, first, start in ((lead_ref, 0, 0), (tail_ref, TILE - 2, width - TILE)):
        block = tile_ref[:, pl.ds(start, TILE), :].astype(F32).reshape(rows * TILE, channels)
        for h in range(channels // LANES):
            flat_ref[h] = block[:, h * LANES : (h + 1) * LANES]
        for x in range(2):
            here = pl.ds(first + x, rows, stride=TILE)
            column = [flat_ref[h, here, :] for h in range(channels // LANES)]
            out_ref[x] = jnp.concatenate(column, axis=1).astype(BF16)
    whole = width // TILE
    rim_ref[0 : 2 * whole] = tile_ref[rows - 2 : rows].reshape(2 * whole, TILE, channels)
    rim_ref[2 * whole :] = tile_ref[0:1].reshape(whole, TILE, channels)


def down_kernel(rim_ref, left_ref, right_ref, lead_ref, tail_ref, down_ref):
    rows = left_ref.shape[1]
    parts = (left_ref, left_ref, lead_ref, tail_ref, right_ref, right_ref)
    count = down_ref.shape[0] - len(parts)
    down_ref[0:count] = rim_ref[0:count]
    for i, part in enumerate(parts):
        down_ref[count + i] = part[i % 2, rows - TILE : rows]


def up_kernel(rim_ref, left_ref, right_ref, lead_ref, tail_ref, sides_ref, up_ref):
    parts = (left_ref, left_ref, lead_ref, tail_ref, right_ref, right_ref)
    count = up_ref.shape[0] - len(parts)
    up_ref[0:count] = rim_ref[2 * count : 3 * count]
    for i, part in enumerate(parts):
        sides_ref[i] = part[i % 2]
        up_ref[count + i] = part[i % 2, 0:TILE]


def exchange(features, later):
    rows, cols, channels = features.shape
    vmem = pl.BlockSpec(memory_space=pltpu.VMEM)
    below = shift(features, "row", -1)
    whole = cols // TILE
    pair = jax.ShapeDtypeStruct((2, rows, channels), BF16)
    rim = jax.ShapeDtypeStruct((3 * whole, TILE, channels), BF16)
    lead, tail, rim = call(
        columns_kernel, (pair, pair, rim), [vmem],
        [pltpu.VMEM((channels // LANES, rows * TILE, LANES), F32)], 4, 10**5, features,
    )
    left = shift(tail, "col", 1)
    right = shift(lead, "col", -1)
    strips = (rim, left, right, lead, tail)
    (to_down,) = call(
        down_kernel, (jax.ShapeDtypeStruct((2 * whole + 6, TILE, channels), BF16),),
        [vmem] * 5, [], 4, 10**5, *strips,
    )
    above, later = lax.optimization_barrier((shift(to_down, "row", 1), later))
    sides_shape = jax.ShapeDtypeStruct((6, rows, channels), BF16)
    up_shape = jax.ShapeDtypeStruct((whole + 6, TILE, channels), BF16)
    own_sides, to_up = call(
        up_kernel, (sides_shape, up_shape), [vmem] * 5, [], 4, 10**5, *strips
    )
    sides = shift(own_sides, "row", -1)
    after = shift(to_up, "row", -2)
    return below, own_sides, sides, above, after, later


def sample(lower, extent):
    lower_f = lower.astype(F32)[:, None]
    extent_f = extent.astype(F32)[:, None]
    bins = jnp.arange(POOL).astype(F32)[None, :]
    centre = lower_f + (bins + 0.5) * extent_f / POOL - 0.5
    return jnp.clip(centre, lower_f, lower_f + extent_f - 1.0)


def spread(dst, start, value, edge_ref, sides, offset):
    count, width, channels = value.shape
    place = lax.broadcasted_iota(jnp.int32, (width, channels), 0)
    for k in range(count):
        line = value[k].astype(F32)
        low = edge_ref[sides[0], pl.ds(offset + k, 1), :]
        high = edge_ref[sides[1], pl.ds(offset + k, 1), :]
        before = jnp.where(place == 0, low, pltpu.roll(line, 1, 0))
        after = jnp.where(place == width - 1, high, pltpu.roll(line, width - 1, 0))
        dst[start + k, :, 0:channels] = before.astype(BF16)
        dst[start + k, :, channels : 2 * channels] = line.astype(BF16)
        dst[start + k, :, 2 * channels : 3 * channels] = after.astype(BF16)


def taps(src, start, count, weight, bias):
    width, depth = src.shape[1:]
    parts = [src[pl.ds(start + d, count)].reshape(count * width, depth) for d in range(3)]
    out = jnp.dot(jnp.concatenate(parts, axis=1), weight, preferred_element_type=F32)
    out = jnp.maximum(out + bias, 0.0)
    return out.reshape(count, width, out.shape[-1])


def main_kernel(
    flags_ref, hit_ref, at_ref, by_ref,
    own_ref, below_ref, own_sides_ref, sides_ref, above_ref, after_ref,
    weight_ref, bias_ref,
    tower_ref, mine_ref, other_ref,
    wide_ref, mid_ref, band_ref, comb_ref, patch_ref, strip_ref, inner_ref,
):
    rows, width, channels = own_ref.shape
    half = mine_ref.shape[0]
    whole = width // TILE
    for c in range(6):
        strip_ref[c, 0:2, :] = above_ref[2 * whole + c].astype(F32)[TILE - 2 : TILE]
        strip_ref[c, 2 : rows + 2, :] = own_sides_ref[c].astype(F32)
        strip_ref[c, rows + 2 : 2 * rows + 2, :] = sides_ref[c].astype(F32)
        strip_ref[c, 2 * rows + 2 : 2 * rows + 3, :] = after_ref[whole + c].astype(F32)[0:1]
        tail = strip_ref.shape[1] - (2 * rows + 3)
        strip_ref[c, 2 * rows + 3 :, :] = jnp.zeros((tail, channels), F32)
    spread(wide_ref, 0, above_ref[0 : 2 * whole].reshape(2, width, channels), strip_ref, (1, 4), 0)
    step = 8
    for part, base in ((own_ref, 2), (below_ref, 2 + rows)):
        def fill(i, carry):
            at = i * step
            spread(wide_ref, base + at, part[pl.ds(at, step)], strip_ref, (1, 4), base + at)
            return carry

        lax.fori_loop(0, rows // step, fill, 0)
    last = 2 + 2 * rows
    spread(wide_ref, last, after_ref[0:whole].reshape(1, width, channels), strip_ref, (1, 4), last)
    wide_ref[3 + 2 * rows] = jnp.zeros(wide_ref.shape[1:], BF16)

    tall = inner_ref.shape[1]
    sides = []
    for side in range(2):
        parts = [
            strip_ref[3 * side + dx, dy : dy + tall, :].astype(BF16)
            for dy in range(3)
            for dx in range(3)
        ]
        sides.append(jnp.concatenate(parts, axis=1))
    out = jnp.dot(jnp.concatenate(sides, axis=0), weight_ref[0], preferred_element_type=F32)
    out = jnp.maximum(out + bias_ref[0:1], 0.0).astype(BF16).astype(F32)
    for side in range(2):
        part = out[side * tall : (side + 1) * tall]
        inner_ref[side] = jnp.where(flags_ref[2 + side] > 0, part, 0.0)

    def first(i, carry):
        at = i * FIRST
        out = taps(wide_ref, at, FIRST, weight_ref[0], bias_ref[0:1])
        spread(mid_ref, at, out.astype(BF16), inner_ref, (0, 1), at)
        return carry

    lax.fori_loop(0, (2 * rows + 2) // FIRST, first, 0)
    blank = jnp.zeros(mid_ref.shape[1:], BF16)

    @pl.when(flags_ref[0] > 0)
    def _():
        mid_ref[0] = blank

    @pl.when(flags_ref[1] > 0)
    def _():
        mid_ref[rows + 1] = blank
    mid_ref[2 * rows + 1] = blank

    def second(i, carry):
        at = i * SECOND
        out = taps(mid_ref, at, SECOND, weight_ref[1], bias_ref[1:2])

        @pl.when(at < rows)
        def _():
            tower_ref[pl.ds(at, SECOND)] = out.astype(BF16)

        band_ref[pl.ds(at, SECOND)] = out.astype(BF16).astype(F32)
        return carry

    lax.fori_loop(0, 2 * rows // SECOND, second, 0)
    halves = [(h, slice(h * LANES, (h + 1) * LANES)) for h in range(channels // LANES)]
    for side, out_ref in ((1, other_ref), (0, mine_ref)):
        def region(m, carry):
            n = m + side * half

            @pl.when(hit_ref[n] > 0)
            def _():
                for p in range(POOL):
                    line = band_ref[at_ref[0, n, p]] * by_ref[0, n, p]
                    line = line + band_ref[at_ref[1, n, p]] * by_ref[1, n, p]
                    for h, lanes in halves:
                        comb_ref[h, pl.ds(p, width, stride=SIDE), :] = line[:, lanes]
                for q in range(POOL):
                    low = pl.ds(pl.multiple_of(at_ref[2, n, q] * SIDE, SIDE), SIDE)
                    high = pl.ds(pl.multiple_of(at_ref[3, n, q] * SIDE, SIDE), SIDE)
                    for h, lanes in halves:
                        total = comb_ref[h, low, :] * by_ref[2, n, q]
                        total = total + comb_ref[h, high, :] * by_ref[3, n, q]
                        patch_ref[h, pl.ds(q, SIDE, stride=POOL), :] = total
                for h, lanes in halves:
                    out_ref[m, :, lanes] = patch_ref[h, pl.ds(0, POOL * POOL), :].astype(BF16)

            @pl.when(hit_ref[n] == 0)
            def _():
                out_ref[m] = jnp.zeros(out_ref.shape[1:], BF16)

            return carry

        lax.fori_loop(0, half, region, 0)


def taps_of(boxes, rows, cols):
    row_first = lax.axis_index("row") * rows
    col_first = lax.axis_index("col") * cols
    at, by = [], []
    for dim, start, size in ((0, row_first, 2 * rows), (1, col_first, cols)):
        centre = sample(boxes[:, dim], boxes[:, dim + 2])
        low = jnp.floor(centre)
        for place in (low, low + 1.0):
            weight = jnp.maximum(1.0 - jnp.abs(place - centre), 0.0).astype(BF16).astype(F32)
            index = place.astype(jnp.int32) - start
            at.append(jnp.clip(index, 0, size - 1))
            by.append(jnp.where((index >= 0) & (index < size), weight, 0.0))
    hit = (boxes[:, 1] < col_first + cols) & (boxes[:, 1] + boxes[:, 3] > col_first)
    return hit.astype(jnp.int32), jnp.stack(at), jnp.stack(by)


def stage_kernel(src_ref, dst_ref, sem):
    load = pltpu.make_async_copy(src_ref, dst_ref, sem)
    load.start()
    load.wait()


def tower_and_pool(features, weight, bias, boxes, owner_slot, wanted):
    rows, cols, channels = features.shape
    below, own_sides, sides, above, after, (boxes, owner_slot, wanted, weight) = exchange(
        features, (boxes, owner_slot, wanted, weight.reshape(2, -1, weight.shape[-1]))
    )
    (weight,) = call(
        stage_kernel, (jax.ShapeDtypeStruct(weight.shape, BF16),),
        [pl.BlockSpec(memory_space=pl.ANY)], [pltpu.SemaphoreType.DMA], 4, 10**5, weight,
    )
    row, col = lax.axis_index("row"), lax.axis_index("col")
    last_row, last_col = lax.axis_size("row") - 1, lax.axis_size("col") - 1
    flags = jnp.stack([row == 0, row == last_row, col > 0, col < last_col]).astype(jnp.int32)
    picked = (owner_slot[0][None, :] == wanted[:, None]).astype(jnp.int32)
    boxes = jnp.sum(picked[:, :, None] * boxes[None, :, :], axis=1)
    hit, at, by = taps_of(boxes, rows, cols)
    count = boxes.shape[0]
    smem = pl.BlockSpec(memory_space=pltpu.SMEM)
    vmem = pl.BlockSpec(memory_space=pltpu.VMEM)
    patches = jax.ShapeDtypeStruct((count // 2, POOL * POOL, channels), BF16)
    return call(
        main_kernel,
        (jax.ShapeDtypeStruct(features.shape, BF16), patches, patches),
        [smem] * 4 + [vmem] * 8,
        [
            pltpu.VMEM((2 * rows + 4, cols, 3 * channels), BF16),
            pltpu.VMEM((2 * rows + 2, cols, 3 * channels), BF16),
            pltpu.VMEM((2 * rows, cols, channels), F32),
            pltpu.VMEM((channels // LANES, cols * SIDE, LANES), F32),
            pltpu.VMEM((channels // LANES, SIDE * SIDE, LANES), F32),
            pltpu.VMEM((6, 2 * rows + 24, channels), F32),
            pltpu.VMEM((2, 2 * rows + 16, channels), F32),
        ],
        40, 6 * 10**9,
        flags, hit, at, by, features, below, own_sides, sides, above, after,
        weight, bias,
    )


def head_kernel(
    mine_ref, swapped_ref, ahead_ref, three_ref, two_ref,
    weight_ref, bias_ref, lift_ref, shade_ref,
    out_ref, sum_ref, wide_ref, row_ref,
):
    channels = bias_ref.shape[-1]
    halves = [(h, slice(h * LANES, (h + 1) * LANES)) for h in range(channels // LANES)]
    parts = (mine_ref[7], swapped_ref[7], ahead_ref[1], three_ref[...], two_ref[...])
    pooled = sum(part.astype(F32) for part in parts).astype(BF16).astype(F32)
    for h, lanes in halves:
        sum_ref[h, 8 : 8 + POOL * POOL, :] = pooled[:, lanes]
    blank = jnp.zeros(wide_ref.shape[1:], BF16)
    wide_ref[0] = blank
    wide_ref[POOL + 1] = blank
    place = lax.broadcasted_iota(jnp.int32, (SIDE, LANES), 0)
    for p in range(POOL):
        for d in range(3):
            kept = (place + d - 1 >= 0) & (place + d - 1 < POOL)
            for h in range(channels // LANES):
                value = sum_ref[h, pl.ds(8 + POOL * p + d - 1, SIDE), :]
                first = d * channels + h * LANES
                wide_ref[p + 1, :, first : first + LANES] = jnp.where(kept, value, 0.0).astype(BF16)
    hidden = taps(wide_ref, 0, POOL, weight_ref[...], bias_ref[...]).astype(BF16)
    hidden = hidden.reshape(POOL * SIDE, channels)
    for u in range(2):
        lifted = []
        for v in range(2):
            value = jnp.dot(hidden, lift_ref[2 * u + v], preferred_element_type=F32)
            lifted.append(jnp.maximum(value + shade_ref[...], 0.0))
        for a in range(POOL):
            for v in range(2):
                for h, lanes in halves:
                    row_ref[a, h, pl.ds(v, SIDE, stride=2), :] = lifted[v][
                        a * SIDE : (a + 1) * SIDE, lanes
                    ]
            for h, lanes in halves:
                out_ref[0, 2 * a + u, :, lanes] = row_ref[a, h, 0 : 2 * POOL, :].astype(BF16)


def head(parts, mask_weight, mask_bias, deconv_weight, deconv_bias):
    channels = mask_bias.shape[-1]
    vmem = pl.BlockSpec(memory_space=pltpu.VMEM)
    side = 2 * POOL
    (masks,) = call(
        head_kernel,
        (jax.ShapeDtypeStruct((1, side, side, channels), BF16),),
        [vmem] * 9,
        [
            pltpu.VMEM((channels // LANES, 8 + SIDE * SIDE, LANES), F32),
            pltpu.VMEM((SIDE, SIDE, 3 * channels), BF16),
            pltpu.VMEM((POOL, channels // LANES, 2 * SIDE, LANES), F32),
        ],
        16, 10**9,
        *parts, mask_weight.reshape(9 * channels, channels), mask_bias,
        deconv_weight.reshape(4, channels, channels), deconv_bias.reshape(1, channels),
    )
    return masks


def per_device(
    features, tower_weight, tower_bias, boxes, owner_slot,
    mask_weight, mask_bias, deconv_weight, deconv_bias,
):
    peers = lax.axis_size("col")
    chips = peers // 2
    core = lax.axis_index("col") % 2
    chip = lax.axis_index("col") // 2
    hops = jnp.array(HOPS * 2, dtype=jnp.int32)
    sides = jnp.repeat(jnp.stack([core, 1 - core]), chips)
    wanted = 2 * ((chip + hops * (1 - 2 * sides)) % chips) + sides
    tower, mine, other = tower_and_pool(
        features, tower_weight, tower_bias, boxes, owner_slot, wanted
    )
    swapped = lax.ppermute(other, "col", [(i, i ^ 1) for i in range(peers)])

    def send(value, hop):
        steps = [2 * hop * (1 - 2 * (i % 2)) for i in range(peers)]
        return lax.ppermute(value, "col", [(i, (i + steps[i]) % peers) for i in range(peers)])

    def total(*parts):
        parts = [part.astype(F32) for part in parts]
        return sum(parts[1:], parts[0]).astype(BF16)

    ahead = send(total(mine[0:3], swapped[0:3]), 1)
    back = send(total(mine[3:5], swapped[3:5]), -1)
    three = send(total(mine[5], swapped[5], ahead[0], back[0]), 3)
    two = send(total(mine[6], swapped[6], ahead[2], back[1]), -2)
    parts = (mine, swapped, ahead, three, two)
    masks = head(parts, mask_weight, mask_bias, deconv_weight, deconv_bias)
    return tower, masks


def solution(mesh):
    placed = (P("row", "col", None), P(), P(), P("row", None), P("row", None), P(), P(), P(), P())
    return jax.shard_map(
        per_device,
        mesh=mesh,
        in_specs=placed,
        out_specs=(P("row", "col", None), P(("row", "col"), None, None, None)),
        check_vma=False,
    )
```

```python
import functools

import jax
import jax.numpy as jnp
from jax import lax
from jax.experimental import pallas as pl
from jax.experimental.pallas import tpu as pltpu
from jax.sharding import PartitionSpec as P

POOL = 14
SIDE = 16
LANES = 128
TILE = 16
FIRST = 33
SECOND = 32
HOPS = (4, 1, -1, 2, -3, 3, -2, 0)
F32 = jnp.float32
BF16 = jnp.bfloat16


def shift(value, axis, step):
    devices = range(lax.axis_size(axis))
    return lax.ppermute(value, axis, [(i, i + step) for i in devices if i + step in devices])


def call(kernel, out_shape, in_specs, scratch, limit, flops, *args):
    vmem = pl.BlockSpec(memory_space=pltpu.VMEM)
    return pl.pallas_call(
        kernel,
        out_shape=out_shape,
        in_specs=in_specs,
        out_specs=tuple(vmem for _ in out_shape),
        scratch_shapes=scratch,
        compiler_params=pltpu.CompilerParams(vmem_limit_bytes=limit * 2**20),
        cost_estimate=pl.CostEstimate(flops=flops, bytes_accessed=10**6, transcendentals=0),
    )(*args)


def columns_kernel(tile_ref, lead_ref, tail_ref, rim_ref, flat_ref):
    rows, width, channels = tile_ref.shape
    for out_ref, first, start in ((lead_ref, 0, 0), (tail_ref, TILE - 2, width - TILE)):
        block = tile_ref[:, pl.ds(start, TILE), :].astype(F32).reshape(rows * TILE, channels)
        for h in range(channels // LANES):
            flat_ref[h] = block[:, h * LANES : (h + 1) * LANES]
        for x in range(2):
            here = pl.ds(first + x, rows, stride=TILE)
            column = [flat_ref[h, here, :] for h in range(channels // LANES)]
            out_ref[x] = jnp.concatenate(column, axis=1).astype(BF16)
    whole = width // TILE
    rim_ref[0 : 2 * whole] = tile_ref[rows - 2 : rows].reshape(2 * whole, TILE, channels)
    rim_ref[2 * whole :] = tile_ref[0:1].reshape(whole, TILE, channels)


def down_kernel(rim_ref, left_ref, right_ref, lead_ref, tail_ref, down_ref):
    rows = left_ref.shape[1]
    parts = (left_ref, left_ref, lead_ref, tail_ref, right_ref, right_ref)
    count = down_ref.shape[0] - len(parts)
    down_ref[0:count] = rim_ref[0:count]
    for i, part in enumerate(parts):
        down_ref[count + i] = part[i % 2, rows - TILE : rows]


def up_kernel(rim_ref, left_ref, right_ref, lead_ref, tail_ref, sides_ref, up_ref):
    parts = (left_ref, left_ref, lead_ref, tail_ref, right_ref, right_ref)
    count = up_ref.shape[0] - len(parts)
    up_ref[0:count] = rim_ref[2 * count : 3 * count]
    for i, part in enumerate(parts):
        sides_ref[i] = part[i % 2]
        up_ref[count + i] = part[i % 2, 0:TILE]


def exchange(features):
    rows, cols, channels = features.shape
    vmem = pl.BlockSpec(memory_space=pltpu.VMEM)
    below = shift(features, "row", -1)
    whole = cols // TILE
    pair = jax.ShapeDtypeStruct((2, rows, channels), BF16)
    rim = jax.ShapeDtypeStruct((3 * whole, TILE, channels), BF16)
    lead, tail, rim = call(
        columns_kernel, (pair, pair, rim), [vmem],
        [pltpu.VMEM((channels // LANES, rows * TILE, LANES), F32)], 4, 10**5, features,
    )
    left = shift(tail, "col", 1)
    right = shift(lead, "col", -1)
    strips = (rim, left, right, lead, tail)
    (to_down,) = call(
        down_kernel, (jax.ShapeDtypeStruct((2 * whole + 6, TILE, channels), BF16),),
        [vmem] * 5, [], 4, 10**5, *strips,
    )
    above = shift(to_down, "row", 1)
    sides_shape = jax.ShapeDtypeStruct((6, rows, channels), BF16)
    up_shape = jax.ShapeDtypeStruct((whole + 6, TILE, channels), BF16)
    own_sides, to_up = call(
        up_kernel, (sides_shape, up_shape), [vmem] * 5, [], 4, 10**5, *strips
    )
    sides = shift(own_sides, "row", -1)
    after = shift(to_up, "row", -2)
    return below, own_sides, sides, above, after


def plan_kernel(boxes_ref, owner_ref, at_ref, by_ref, *, rows, cols, axes):
    row, col = lax.axis_index("row"), lax.axis_index("col")
    count = boxes_ref.shape[0]
    chips = axes[1] // 2
    slot = lax.broadcasted_iota(jnp.int32, (count, LANES), 0)
    bins = lax.broadcasted_iota(jnp.int32, (count, LANES), 1).astype(F32)
    core = jnp.where(slot < chips, col % 2, 1 - col % 2)
    hop = jnp.zeros_like(slot)
    for i, step in enumerate(HOPS):
        hop = jnp.where((slot == i) | (slot == i + chips), step, hop)
    chip = col // 2 + hop * (1 - 2 * core) + chips
    chip = jnp.where(chip >= chips, chip - chips, chip)
    chip = jnp.where(chip >= chips, chip - chips, chip)
    wanted = 2 * chip + core
    fields = [jnp.zeros_like(slot) for _ in range(4)]
    for k in range(count):
        here = wanted == owner_ref[0, k]
        fields = [jnp.where(here, boxes_ref[k, f], fields[f]) for f in range(4)]
    for dim, start, size in ((0, row * rows, 2 * rows), (1, col * cols, cols)):
        lower, extent = fields[dim].astype(F32), fields[dim + 2].astype(F32)
        centre = lower + (bins + 0.5) * extent / POOL - 0.5
        centre = jnp.minimum(jnp.maximum(centre, lower), lower + extent - 1.0)
        low = jnp.floor(centre)
        for t, place in enumerate((low, low + 1.0)):
            weight = jnp.maximum(1.0 - jnp.abs(place - centre), 0.0).astype(BF16).astype(F32)
            index = place.astype(jnp.int32) - start
            inside = (index >= 0) & (index < size)
            at = jnp.minimum(jnp.maximum(index, 0), size - 1)
            at_ref[2 * dim + t] = at[:, :POOL]
            by_ref[2 * dim + t] = jnp.where(inside, weight, 0.0)[:, :POOL]
    left, right = fields[1], fields[1] + fields[3]
    hit = (left < (col + 1) * cols) & (right > col * cols)
    at_ref[4] = jnp.where(hit, 1, 0)[:, :POOL]


def spread(dst, start, value, edge_ref, sides, offset):
    count, width, channels = value.shape
    place = lax.broadcasted_iota(jnp.int32, (width, channels), 0)
    for k in range(count):
        line = value[k].astype(F32)
        low = edge_ref[sides[0], pl.ds(offset + k, 1), :]
        high = edge_ref[sides[1], pl.ds(offset + k, 1), :]
        before = jnp.where(place == 0, low, pltpu.roll(line, 1, 0))
        after = jnp.where(place == width - 1, high, pltpu.roll(line, width - 1, 0))
        dst[start + k, :, 0:channels] = before.astype(BF16)
        dst[start + k, :, channels : 2 * channels] = line.astype(BF16)
        dst[start + k, :, 2 * channels : 3 * channels] = after.astype(BF16)


def taps(src, start, count, weight, bias):
    width, depth = src.shape[1:]
    parts = [src[pl.ds(start + d, count)].reshape(count * width, depth) for d in range(3)]
    out = jnp.dot(jnp.concatenate(parts, axis=1), weight, preferred_element_type=F32)
    out = jnp.maximum(out + bias, 0.0)
    return out.reshape(count, width, out.shape[-1])


def main_kernel(
    at_ref, by_ref,
    own_ref, below_ref, own_sides_ref, sides_ref, above_ref, after_ref,
    weight_hbm, bias_ref,
    tower_ref, mine_ref, other_ref,
    wide_ref, mid_ref, band_ref, comb_ref, patch_ref, strip_ref, inner_ref, weight_ref, sems, *, last_row, last_col,
):
    rows, width, channels = own_ref.shape
    half = mine_ref.shape[0]
    whole = width // TILE
    loads = [
        pltpu.make_async_copy(weight_hbm.at[l], weight_ref.at[l], sems.at[l]) for l in range(2)
    ]
    for load in loads:
        load.start()
    row, col = lax.axis_index("row"), lax.axis_index("col")
    for c in range(6):
        strip_ref[c, 0:2, :] = above_ref[2 * whole + c].astype(F32)[TILE - 2 : TILE]
        strip_ref[c, 2 : rows + 2, :] = own_sides_ref[c].astype(F32)
        strip_ref[c, rows + 2 : 2 * rows + 2, :] = sides_ref[c].astype(F32)
        strip_ref[c, 2 * rows + 2 : 2 * rows + 3, :] = after_ref[whole + c].astype(F32)[0:1]
        tail = strip_ref.shape[1] - (2 * rows + 3)
        strip_ref[c, 2 * rows + 3 :, :] = jnp.zeros((tail, channels), F32)
    spread(wide_ref, 0, above_ref[0 : 2 * whole].reshape(2, width, channels), strip_ref, (1, 4), 0)
    step = 8
    for part, base in ((own_ref, 2), (below_ref, 2 + rows)):
        def fill(i, carry):
            at = i * step
            spread(wide_ref, base + at, part[pl.ds(at, step)], strip_ref, (1, 4), base + at)
            return carry

        lax.fori_loop(0, rows // step, fill, 0)
    last = 2 + 2 * rows
    spread(wide_ref, last, after_ref[0:whole].reshape(1, width, channels), strip_ref, (1, 4), last)
    wide_ref[3 + 2 * rows] = jnp.zeros(wide_ref.shape[1:], BF16)

    loads[0].wait()
    tall = inner_ref.shape[1]
    sides = []
    for side in range(2):
        parts = [
            strip_ref[3 * side + dx, dy : dy + tall, :].astype(BF16)
            for dy in range(3)
            for dx in range(3)
        ]
        sides.append(jnp.concatenate(parts, axis=1))
    out = jnp.dot(jnp.concatenate(sides, axis=0), weight_ref[0], preferred_element_type=F32)
    out = jnp.maximum(out + bias_ref[0:1], 0.0).astype(BF16).astype(F32)
    for side in range(2):
        part = out[side * tall : (side + 1) * tall]
        inner_ref[side] = jnp.where((col > 0) if side == 0 else (col < last_col), part, 0.0)

    def first(i, carry):
        at = i * FIRST
        out = taps(wide_ref, at, FIRST, weight_ref[0], bias_ref[0:1])
        spread(mid_ref, at, out.astype(BF16), inner_ref, (0, 1), at)
        return carry

    lax.fori_loop(0, (2 * rows + 2) // FIRST, first, 0)
    blank = jnp.zeros(mid_ref.shape[1:], BF16)

    @pl.when(row == 0)
    def _():
        mid_ref[0] = blank

    @pl.when(row == last_row)
    def _():
        mid_ref[rows + 1] = blank
    mid_ref[2 * rows + 1] = blank

    loads[1].wait()

    def second(i, carry):
        at = i * SECOND
        out = taps(mid_ref, at, SECOND, weight_ref[1], bias_ref[1:2])

        @pl.when(at < rows)
        def _():
            tower_ref[pl.ds(at, SECOND)] = out.astype(BF16)

        band_ref[pl.ds(at, SECOND)] = out.astype(BF16).astype(F32)
        return carry

    lax.fori_loop(0, 2 * rows // SECOND, second, 0)
    halves = [(h, slice(h * LANES, (h + 1) * LANES)) for h in range(channels // LANES)]
    for side, out_ref in ((1, other_ref), (0, mine_ref)):
        def region(m, carry):
            n = m + side * half

            @pl.when(at_ref[4, n, 0] > 0)
            def _():
                for p in range(POOL):
                    line = band_ref[at_ref[0, n, p]] * by_ref[0, n, p]
                    line = line + band_ref[at_ref[1, n, p]] * by_ref[1, n, p]
                    for h, lanes in halves:
                        comb_ref[h, pl.ds(p, width, stride=SIDE), :] = line[:, lanes]
                for q in range(POOL):
                    low = pl.ds(pl.multiple_of(at_ref[2, n, q] * SIDE, SIDE), SIDE)
                    high = pl.ds(pl.multiple_of(at_ref[3, n, q] * SIDE, SIDE), SIDE)
                    for h, lanes in halves:
                        total = comb_ref[h, low, :] * by_ref[2, n, q]
                        total = total + comb_ref[h, high, :] * by_ref[3, n, q]
                        patch_ref[h, pl.ds(q, SIDE, stride=POOL), :] = total
                for h, lanes in halves:
                    out_ref[m, :, lanes] = patch_ref[h, pl.ds(0, POOL * POOL), :].astype(BF16)

            @pl.when(at_ref[4, n, 0] == 0)
            def _():
                out_ref[m] = jnp.zeros(out_ref.shape[1:], BF16)

            return carry

        lax.fori_loop(0, half, region, 0)


def tower_and_pool(features, weight, bias, boxes, owner_slot):
    rows, cols, channels = features.shape
    below, own_sides, sides, above, after = exchange(features)
    above, boxes = lax.optimization_barrier((above, boxes))
    count = boxes.shape[0]
    smem = pl.BlockSpec(memory_space=pltpu.SMEM)
    vmem = pl.BlockSpec(memory_space=pltpu.VMEM)
    at, by = call(
        functools.partial(
            plan_kernel, rows=rows, cols=cols, axes=(lax.axis_size("row"), lax.axis_size("col"))
        ),
        (
            jax.ShapeDtypeStruct((5, count, POOL), jnp.int32),
            jax.ShapeDtypeStruct((4, count, POOL), F32),
        ),
        [smem, smem], [], 4, 10**5, boxes, owner_slot,
    )
    patches = jax.ShapeDtypeStruct((count // 2, POOL * POOL, channels), BF16)
    kernel = functools.partial(
        main_kernel, last_row=lax.axis_size("row") - 1, last_col=lax.axis_size("col") - 1
    )
    return call(
        kernel,
        (jax.ShapeDtypeStruct(features.shape, BF16), patches, patches),
        [smem] * 2 + [vmem] * 6 + [pl.BlockSpec(memory_space=pl.ANY), vmem],
        [
            pltpu.VMEM((2 * rows + 4, cols, 3 * channels), BF16),
            pltpu.VMEM((2 * rows + 2, cols, 3 * channels), BF16),
            pltpu.VMEM((2 * rows, cols, channels), F32),
            pltpu.VMEM((channels // LANES, cols * SIDE, LANES), F32),
            pltpu.VMEM((channels // LANES, SIDE * SIDE, LANES), F32),
            pltpu.VMEM((6, 2 * rows + 24, channels), F32),
            pltpu.VMEM((2, 2 * rows + 16, channels), F32),
            pltpu.VMEM((2, 9 * channels, channels), BF16),
            pltpu.SemaphoreType.DMA((2,)),
        ],
        51, 6 * 10**9,
        at, by, features, below, own_sides, sides, above, after,
        weight.reshape(2, 9 * channels, channels), bias,
    )


def head_kernel(
    mine_ref, swapped_ref, ahead_ref, three_ref, two_ref,
    weight_ref, bias_ref, lift_ref, shade_ref,
    out_ref, sum_ref, wide_ref, row_ref,
):
    channels = bias_ref.shape[-1]
    halves = [(h, slice(h * LANES, (h + 1) * LANES)) for h in range(channels // LANES)]
    parts = (mine_ref[7], swapped_ref[7], ahead_ref[1], three_ref[...], two_ref[...])
    pooled = sum(part.astype(F32) for part in parts).astype(BF16).astype(F32)
    for h, lanes in halves:
        sum_ref[h, 8 : 8 + POOL * POOL, :] = pooled[:, lanes]
    blank = jnp.zeros(wide_ref.shape[1:], BF16)
    wide_ref[0] = blank
    wide_ref[POOL + 1] = blank
    place = lax.broadcasted_iota(jnp.int32, (SIDE, LANES), 0)
    for p in range(POOL):
        for d in range(3):
            kept = (place + d - 1 >= 0) & (place + d - 1 < POOL)
            for h in range(channels // LANES):
                value = sum_ref[h, pl.ds(8 + POOL * p + d - 1, SIDE), :]
                first = d * channels + h * LANES
                wide_ref[p + 1, :, first : first + LANES] = jnp.where(kept, value, 0.0).astype(BF16)
    hidden = taps(wide_ref, 0, POOL, weight_ref[...], bias_ref[...]).astype(BF16)
    hidden = hidden.reshape(POOL * SIDE, channels)
    for u in range(2):
        lifted = []
        for v in range(2):
            value = jnp.dot(hidden, lift_ref[2 * u + v], preferred_element_type=F32)
            lifted.append(jnp.maximum(value + shade_ref[...], 0.0))
        for a in range(POOL):
            for v in range(2):
                for h, lanes in halves:
                    row_ref[a, h, pl.ds(v, SIDE, stride=2), :] = lifted[v][
                        a * SIDE : (a + 1) * SIDE, lanes
                    ]
            for h, lanes in halves:
                out_ref[0, 2 * a + u, :, lanes] = row_ref[a, h, 0 : 2 * POOL, :].astype(BF16)


def head(parts, mask_weight, mask_bias, deconv_weight, deconv_bias):
    channels = mask_bias.shape[-1]
    vmem = pl.BlockSpec(memory_space=pltpu.VMEM)
    side = 2 * POOL
    (masks,) = call(
        head_kernel,
        (jax.ShapeDtypeStruct((1, side, side, channels), BF16),),
        [vmem] * 9,
        [
            pltpu.VMEM((channels // LANES, 8 + SIDE * SIDE, LANES), F32),
            pltpu.VMEM((SIDE, SIDE, 3 * channels), BF16),
            pltpu.VMEM((POOL, channels // LANES, 2 * SIDE, LANES), F32),
        ],
        16, 10**9,
        *parts, mask_weight.reshape(9 * channels, channels), mask_bias,
        deconv_weight.reshape(4, channels, channels), deconv_bias.reshape(1, channels),
    )
    return masks


def per_device(
    features, tower_weight, tower_bias, boxes, owner_slot,
    mask_weight, mask_bias, deconv_weight, deconv_bias,
):
    peers = lax.axis_size("col")
    chips = peers // 2
    tower, mine, other = tower_and_pool(features, tower_weight, tower_bias, boxes, owner_slot)
    swapped = lax.ppermute(other, "col", [(i, i ^ 1) for i in range(peers)])

    def send(value, hop):
        steps = [2 * hop * (1 - 2 * (i % 2)) for i in range(peers)]
        return lax.ppermute(value, "col", [(i, (i + steps[i]) % peers) for i in range(peers)])

    def total(*parts):
        parts = [part.astype(F32) for part in parts]
        return sum(parts[1:], parts[0]).astype(BF16)

    ahead = send(total(mine[0:3], swapped[0:3]), 1)
    back = send(total(mine[3:5], swapped[3:5]), -1)
    three = send(total(mine[5], swapped[5], ahead[0], back[0]), 3)
    two = send(total(mine[6], swapped[6], ahead[2], back[1]), -2)
    parts = (mine, swapped, ahead, three, two)
    masks = head(parts, mask_weight, mask_bias, deconv_weight, deconv_bias)
    return tower, masks


def solution(mesh):
    placed = (P("row", "col", None), P(), P(), P("row", None), P("row", None), P(), P(), P(), P())
    return jax.shard_map(
        per_device,
        mesh=mesh,
        in_specs=placed,
        out_specs=(P("row", "col", None), P(("row", "col"), None, None, None)),
        check_vma=False,
    )
```

```python
import functools

import jax
import jax.numpy as jnp
from jax import lax
from jax.experimental import pallas as pl
from jax.experimental.pallas import tpu as pltpu
from jax.sharding import PartitionSpec as P

POOL = 14
SIDE = 16
LANES = 128
PATCH = 200
TILE = 16
FIRST = 33
SECOND = 32
HOPS = (4, 1, -1, 2, -3, 3, -2, 0)
F32 = jnp.float32
BF16 = jnp.bfloat16


def shift(value, axis, step):
    devices = range(lax.axis_size(axis))
    return lax.ppermute(value, axis, [(i, i + step) for i in devices if i + step in devices])


def call(kernel, out_shape, in_specs, scratch, limit, flops, *args):
    vmem = pl.BlockSpec(memory_space=pltpu.VMEM)
    return pl.pallas_call(
        kernel,
        out_shape=out_shape,
        in_specs=in_specs,
        out_specs=tuple(vmem for _ in out_shape),
        scratch_shapes=scratch,
        compiler_params=pltpu.CompilerParams(vmem_limit_bytes=limit * 2**20),
        cost_estimate=pl.CostEstimate(flops=flops, bytes_accessed=10**6, transcendentals=0),
    )(*args)


def columns_kernel(
    tile_ref, bias_ref, boxes_ref, owner_ref,
    lead_ref, tail_ref, rim_ref, held_ref, held_bias_ref, held_boxes_ref, held_owner_ref,
    flat_ref,
):
    rows, width, channels = tile_ref.shape
    held_ref[...] = tile_ref[...]
    held_bias_ref[...] = bias_ref[...]
    held_boxes_ref[...] = boxes_ref[...]
    held_owner_ref[...] = owner_ref[...]
    for out_ref, first, start in ((lead_ref, 0, 0), (tail_ref, TILE - 2, width - TILE)):
        block = tile_ref[:, pl.ds(start, TILE), :].astype(F32).reshape(rows * TILE, channels)
        for h in range(channels // LANES):
            flat_ref[h] = block[:, h * LANES : (h + 1) * LANES]
        for x in range(2):
            here = pl.ds(first + x, rows, stride=TILE)
            column = [flat_ref[h, here, :] for h in range(channels // LANES)]
            out_ref[x] = jnp.concatenate(column, axis=1).astype(BF16)
    whole = width // TILE
    rim_ref[0 : 2 * whole] = tile_ref[rows - 2 : rows].reshape(2 * whole, TILE, channels)
    rim_ref[2 * whole :] = tile_ref[0:1].reshape(whole, TILE, channels)


def down_kernel(rim_ref, left_ref, right_ref, lead_ref, tail_ref, down_ref):
    rows = left_ref.shape[1]
    parts = (left_ref, left_ref, lead_ref, tail_ref, right_ref, right_ref)
    count = down_ref.shape[0] - len(parts)
    down_ref[0:count] = rim_ref[0:count]
    for i, part in enumerate(parts):
        down_ref[count + i] = part[i % 2, rows - TILE : rows]


def up_kernel(rim_ref, left_ref, right_ref, lead_ref, tail_ref, sides_ref, up_ref):
    parts = (left_ref, left_ref, lead_ref, tail_ref, right_ref, right_ref)
    count = up_ref.shape[0] - len(parts)
    up_ref[0:count] = rim_ref[2 * count : 3 * count]
    for i, part in enumerate(parts):
        sides_ref[i] = part[i % 2]
        up_ref[count + i] = part[i % 2, 0:TILE]


def exchange(features, *small):
    rows, cols, channels = features.shape
    vmem = pl.BlockSpec(memory_space=pltpu.VMEM)
    below = shift(features, "row", -1)
    whole = cols // TILE
    pair = jax.ShapeDtypeStruct((2, rows, channels), BF16)
    rim = jax.ShapeDtypeStruct((3 * whole, TILE, channels), BF16)
    held = tuple(jax.ShapeDtypeStruct(value.shape, value.dtype) for value in (features,) + small)
    lead, tail, rim, *held = call(
        columns_kernel, (pair, pair, rim) + held, [vmem] * 4,
        [pltpu.VMEM((channels // LANES, rows * TILE, LANES), F32)], 8, 10**5, features, *small,
    )
    left = shift(tail, "col", 1)
    right = shift(lead, "col", -1)
    strips = (rim, left, right, lead, tail)
    (to_down,) = call(
        down_kernel, (jax.ShapeDtypeStruct((2 * whole + 6, TILE, channels), BF16),),
        [vmem] * 5, [], 4, 10**5, *strips,
    )
    above = shift(to_down, "row", 1)
    sides_shape = jax.ShapeDtypeStruct((6, rows, channels), BF16)
    up_shape = jax.ShapeDtypeStruct((whole + 6, TILE, channels), BF16)
    own_sides, to_up = call(
        up_kernel, (sides_shape, up_shape), [vmem] * 5, [], 4, 10**5, *strips
    )
    sides = shift(own_sides, "row", -1)
    after = shift(to_up, "row", -2)
    return below, own_sides, sides, above, after, held


def plan(boxes_ref, owner_ref, at_ref, by_ref, rows, cols, chips):
    row, col = lax.axis_index("row"), lax.axis_index("col")
    count = boxes_ref.shape[1]
    slot = lax.broadcasted_iota(jnp.int32, (count, LANES), 0)
    bins = lax.broadcasted_iota(jnp.int32, (count, LANES), 1).astype(F32)
    core = jnp.where(slot < chips, col % 2, 1 - col % 2)
    hop = jnp.zeros_like(slot)
    for i, step in enumerate(HOPS):
        hop = jnp.where((slot == i) | (slot == i + chips), step, hop)
    chip = col // 2 + hop * (1 - 2 * core) + chips
    chip = jnp.where(chip >= chips, chip - chips, chip)
    chip = jnp.where(chip >= chips, chip - chips, chip)
    wanted = 2 * chip + core
    fields = [jnp.zeros_like(slot) for _ in range(4)]
    for k in range(count):
        here = wanted == owner_ref[0, k]
        fields = [jnp.where(here, boxes_ref[f, k], fields[f]) for f in range(4)]
    for dim, start, size in ((0, row * rows, 2 * rows), (1, col * cols, cols)):
        lower, extent = fields[dim].astype(F32), fields[dim + 2].astype(F32)
        centre = lower + (bins + 0.5) * extent / POOL - 0.5
        centre = jnp.minimum(jnp.maximum(centre, lower), lower + extent - 1.0)
        low = jnp.floor(centre)
        for t, place in enumerate((low, low + 1.0)):
            weight = jnp.maximum(1.0 - jnp.abs(place - centre), 0.0).astype(BF16).astype(F32)
            index = place.astype(jnp.int32) - start
            inside = (index >= 0) & (index < size)
            at = jnp.minimum(jnp.maximum(index, 0), size - 1)
            at_ref[2 * dim + t] = at
            by_ref[2 * dim + t] = jnp.where(inside, weight, 0.0)
    left, right = fields[1], fields[1] + fields[3]
    hit = (left < (col + 1) * cols) & (right > col * cols)
    at_ref[4] = jnp.where(hit, 1, 0)


def spread(dst, start, value, edge_ref, sides, offset):
    count, width, channels = value.shape
    place = lax.broadcasted_iota(jnp.int32, (width, channels), 0)
    for k in range(count):
        line = value[k].astype(F32)
        low = edge_ref[sides[0], pl.ds(offset + k, 1), :]
        high = edge_ref[sides[1], pl.ds(offset + k, 1), :]
        before = jnp.where(place == 0, low, pltpu.roll(line, 1, 0))
        after = jnp.where(place == width - 1, high, pltpu.roll(line, width - 1, 0))
        dst[start + k, :, 0:channels] = before.astype(BF16)
        dst[start + k, :, channels : 2 * channels] = line.astype(BF16)
        dst[start + k, :, 2 * channels : 3 * channels] = after.astype(BF16)


def taps(src, start, count, weight, bias):
    width, depth = src.shape[1:]
    parts = [src[pl.ds(start + d, count)].reshape(count * width, depth) for d in range(3)]
    out = jnp.dot(jnp.concatenate(parts, axis=1), weight, preferred_element_type=F32)
    out = jnp.maximum(out + bias, 0.0)
    return out.reshape(count, width, out.shape[-1])


def main_kernel(
    boxes_ref, owner_ref,
    own_ref, below_ref, own_sides_ref, sides_ref, above_ref, after_ref,
    weight_hbm, bias_ref,
    tower_ref, mine_ref, other_ref,
    wide_ref, mid_ref, band_ref, comb_ref, patch_ref, strip_ref, inner_ref, weight_ref,
    at_tile, by_tile, at_ref, by_ref, sems, *, last_row, last_col,
):
    rows, width, channels = own_ref.shape
    half = mine_ref.shape[0]
    whole = width // TILE
    loads = [
        pltpu.make_async_copy(weight_hbm.at[l], weight_ref.at[l], sems.at[l]) for l in range(2)
    ]
    loads[0].start()
    plan(boxes_ref, owner_ref, at_tile, by_tile, rows, width, (last_col + 1) // 2)
    moves = [
        pltpu.make_async_copy(at_tile, at_ref, sems.at[2]),
        pltpu.make_async_copy(by_tile, by_ref, sems.at[3]),
    ]
    for move in moves:
        move.start()
    row, col = lax.axis_index("row"), lax.axis_index("col")
    for c in range(6):
        strip_ref[c, 0:2, :] = above_ref[2 * whole + c].astype(F32)[TILE - 2 : TILE]
        strip_ref[c, 2 : rows + 2, :] = own_sides_ref[c].astype(F32)
        strip_ref[c, rows + 2 : 2 * rows + 2, :] = sides_ref[c].astype(F32)
        strip_ref[c, 2 * rows + 2 : 2 * rows + 3, :] = after_ref[whole + c].astype(F32)[0:1]
        tail = strip_ref.shape[1] - (2 * rows + 3)
        strip_ref[c, 2 * rows + 3 :, :] = jnp.zeros((tail, channels), F32)
    spread(wide_ref, 0, above_ref[0 : 2 * whole].reshape(2, width, channels), strip_ref, (1, 4), 0)
    step = 8
    for part, base in ((own_ref, 2), (below_ref, 2 + rows)):
        def fill(i, carry):
            at = i * step
            spread(wide_ref, base + at, part[pl.ds(at, step)], strip_ref, (1, 4), base + at)
            return carry

        lax.fori_loop(0, rows // step, fill, 0)
    last = 2 + 2 * rows
    spread(wide_ref, last, after_ref[0:whole].reshape(1, width, channels), strip_ref, (1, 4), last)
    wide_ref[3 + 2 * rows] = jnp.zeros(wide_ref.shape[1:], BF16)

    loads[0].wait()
    loads[1].start()
    tall = inner_ref.shape[1]
    sides = []
    for side in range(2):
        parts = [
            strip_ref[3 * side + dx, dy : dy + tall, :].astype(BF16)
            for dy in range(3)
            for dx in range(3)
        ]
        sides.append(jnp.concatenate(parts, axis=1))
    out = jnp.dot(jnp.concatenate(sides, axis=0), weight_ref[0], preferred_element_type=F32)
    out = jnp.maximum(out + bias_ref[0:1], 0.0).astype(BF16).astype(F32)
    for side in range(2):
        part = out[side * tall : (side + 1) * tall]
        inner_ref[side] = jnp.where((col > 0) if side == 0 else (col < last_col), part, 0.0)

    def first(i, carry):
        at = i * FIRST
        out = taps(wide_ref, at, FIRST, weight_ref[0], bias_ref[0:1])
        spread(mid_ref, at, out.astype(BF16), inner_ref, (0, 1), at)
        return carry

    lax.fori_loop(0, (2 * rows + 2) // FIRST, first, 0)
    blank = jnp.zeros(mid_ref.shape[1:], BF16)

    @pl.when(row == 0)
    def _():
        mid_ref[0] = blank

    @pl.when(row == last_row)
    def _():
        mid_ref[rows + 1] = blank
    mid_ref[2 * rows + 1] = blank

    loads[1].wait()

    def second(i, carry):
        at = i * SECOND
        out = taps(mid_ref, at, SECOND, weight_ref[1], bias_ref[1:2])

        @pl.when(at < rows)
        def _():
            tower_ref[pl.ds(at, SECOND)] = out.astype(BF16)

        band_ref[pl.ds(at, SECOND)] = out.astype(BF16).astype(F32)
        return carry

    lax.fori_loop(0, 2 * rows // SECOND, second, 0)
    for move in moves:
        move.wait()
    halves = [(h, slice(h * LANES, (h + 1) * LANES)) for h in range(channels // LANES)]
    for side, out_ref in ((1, other_ref), (0, mine_ref)):
        def region(m, carry):
            n = m + side * half

            @pl.when(at_ref[4, n, 0] > 0)
            def _():
                for p in range(POOL):
                    line = band_ref[at_ref[0, n, p]] * by_ref[0, n, p]
                    line = line + band_ref[at_ref[1, n, p]] * by_ref[1, n, p]
                    for h, lanes in halves:
                        comb_ref[h, pl.ds(p, width, stride=SIDE), :] = line[:, lanes]
                for q in range(POOL):
                    low = pl.ds(pl.multiple_of(at_ref[2, n, q] * SIDE, SIDE), SIDE)
                    high = pl.ds(pl.multiple_of(at_ref[3, n, q] * SIDE, SIDE), SIDE)
                    for h, lanes in halves:
                        total = comb_ref[h, low, :] * by_ref[2, n, q]
                        total = total + comb_ref[h, high, :] * by_ref[3, n, q]
                        patch_ref[h, pl.ds(q, SIDE, stride=POOL), :] = total
                for h, lanes in halves:
                    out_ref[m, :, lanes] = patch_ref[h, pl.ds(0, PATCH), :].astype(BF16)

            @pl.when(at_ref[4, n, 0] == 0)
            def _():
                out_ref[m] = jnp.zeros(out_ref.shape[1:], BF16)

            return carry

        lax.fori_loop(0, half, region, 0)


def tower_and_pool(features, weight, bias, boxes, owner_slot):
    rows, cols, channels = features.shape
    below, own_sides, sides, above, after, held = exchange(features, bias, boxes.T, owner_slot)
    features, bias, boxes, owner_slot = held
    count = boxes.shape[1]
    smem = pl.BlockSpec(memory_space=pltpu.SMEM)
    vmem = pl.BlockSpec(memory_space=pltpu.VMEM)
    patches = jax.ShapeDtypeStruct((count // 2, PATCH, channels), BF16)
    kernel = functools.partial(
        main_kernel, last_row=lax.axis_size("row") - 1, last_col=lax.axis_size("col") - 1
    )
    return call(
        kernel,
        (jax.ShapeDtypeStruct(features.shape, BF16), patches, patches),
        [smem] * 2 + [vmem] * 6 + [pl.BlockSpec(memory_space=pl.ANY), vmem],
        [
            pltpu.VMEM((2 * rows + 4, cols, 3 * channels), BF16),
            pltpu.VMEM((2 * rows + 2, cols, 3 * channels), BF16),
            pltpu.VMEM((2 * rows, cols, channels), F32),
            pltpu.VMEM((channels // LANES, cols * SIDE, LANES), F32),
            pltpu.VMEM((channels // LANES, SIDE * SIDE, LANES), F32),
            pltpu.VMEM((6, 2 * rows + 24, channels), F32),
            pltpu.VMEM((2, 2 * rows + 16, channels), F32),
            pltpu.VMEM((2, 9 * channels, channels), BF16),
            pltpu.VMEM((5, count, LANES), jnp.int32),
            pltpu.VMEM((4, count, LANES), F32),
            pltpu.SMEM((5, count, LANES), jnp.int32),
            pltpu.SMEM((4, count, LANES), F32),
            pltpu.SemaphoreType.DMA((4,)),
        ],
        51, 6 * 10**9,
        boxes, owner_slot, features, below, own_sides, sides, above, after,
        weight.reshape(2, 9 * channels, channels), bias,
    )


def head_kernel(
    mine_ref, swapped_ref, ahead_ref, three_ref, two_ref,
    weight_ref, bias_ref, lift_ref, shade_ref,
    out_ref, sum_ref, wide_ref, row_ref,
):
    channels = bias_ref.shape[-1]
    halves = [(h, slice(h * LANES, (h + 1) * LANES)) for h in range(channels // LANES)]
    parts = (mine_ref[7], swapped_ref[7], ahead_ref[1], three_ref[...], two_ref[...])
    pooled = sum(part.astype(F32) for part in parts).astype(BF16).astype(F32)
    for h, lanes in halves:
        sum_ref[h, 8 : 8 + PATCH, :] = pooled[:, lanes]
    blank = jnp.zeros(wide_ref.shape[1:], BF16)
    wide_ref[0] = blank
    wide_ref[POOL + 1] = blank
    place = lax.broadcasted_iota(jnp.int32, (SIDE, LANES), 0)
    for p in range(POOL):
        for d in range(3):
            kept = (place + d - 1 >= 0) & (place + d - 1 < POOL)
            for h in range(channels // LANES):
                value = sum_ref[h, pl.ds(8 + POOL * p + d - 1, SIDE), :]
                first = d * channels + h * LANES
                wide_ref[p + 1, :, first : first + LANES] = jnp.where(kept, value, 0.0).astype(BF16)
    hidden = taps(wide_ref, 0, POOL, weight_ref[...], bias_ref[...]).astype(BF16)
    hidden = hidden.reshape(POOL * SIDE, channels)
    for u in range(2):
        lifted = []
        for v in range(2):
            value = jnp.dot(hidden, lift_ref[2 * u + v], preferred_element_type=F32)
            lifted.append(jnp.maximum(value + shade_ref[...], 0.0))
        for a in range(POOL):
            for v in range(2):
                for h, lanes in halves:
                    row_ref[a, h, pl.ds(v, SIDE, stride=2), :] = lifted[v][
                        a * SIDE : (a + 1) * SIDE, lanes
                    ]
            for h, lanes in halves:
                out_ref[0, 2 * a + u, :, lanes] = row_ref[a, h, 0 : 2 * POOL, :].astype(BF16)


def head(parts, mask_weight, mask_bias, deconv_weight, deconv_bias):
    channels = mask_bias.shape[-1]
    vmem = pl.BlockSpec(memory_space=pltpu.VMEM)
    side = 2 * POOL
    (masks,) = call(
        head_kernel,
        (jax.ShapeDtypeStruct((1, side, side, channels), BF16),),
        [vmem] * 9,
        [
            pltpu.VMEM((channels // LANES, 8 + SIDE * SIDE, LANES), F32),
            pltpu.VMEM((SIDE, SIDE, 3 * channels), BF16),
            pltpu.VMEM((POOL, channels // LANES, 2 * SIDE, LANES), F32),
        ],
        16, 10**9,
        *parts, mask_weight.reshape(9 * channels, channels), mask_bias,
        deconv_weight.reshape(4, channels, channels), deconv_bias.reshape(1, channels),
    )
    return masks


def per_device(
    features, tower_weight, tower_bias, boxes, owner_slot,
    mask_weight, mask_bias, deconv_weight, deconv_bias,
):
    peers = lax.axis_size("col")
    chips = peers // 2
    tower, mine, other = tower_and_pool(features, tower_weight, tower_bias, boxes, owner_slot)
    swapped = lax.ppermute(other, "col", [(i, i ^ 1) for i in range(peers)])

    def send(value, hop):
        steps = [2 * hop * (1 - 2 * (i % 2)) for i in range(peers)]
        return lax.ppermute(value, "col", [(i, (i + steps[i]) % peers) for i in range(peers)])

    def total(*parts):
        parts = [part.astype(F32) for part in parts]
        return sum(parts[1:], parts[0]).astype(BF16)

    ahead = send(total(mine[0:3], swapped[0:3]), 1)
    back = send(total(mine[3:5], swapped[3:5]), -1)
    three = send(total(mine[5], swapped[5], ahead[0], back[0]), 3)
    two = send(total(mine[6], swapped[6], ahead[2], back[1]), -2)
    parts = (mine, swapped, ahead, three, two)
    masks = head(parts, mask_weight, mask_bias, deconv_weight, deconv_bias)
    return tower, masks


def solution(mesh):
    placed = (P("row", "col", None), P(), P(), P("row", None), P("row", None), P(), P(), P(), P())
    return jax.shard_map(
        per_device,
        mesh=mesh,
        in_specs=placed,
        out_specs=(P("row", "col", None), P(("row", "col"), None, None, None)),
        check_vma=False,
    )
```

```python
import functools

import jax
import jax.numpy as jnp
from jax import lax
from jax.experimental import pallas as pl
from jax.experimental.pallas import tpu as pltpu
from jax.sharding import PartitionSpec as P

POOL = 14
SIDE = 16
LANES = 128
PATCH = 200
TILE = 16
FIRST = 33
SECOND = 32
HOPS = (4, 1, -1, 2, -3, 3, -2, 0)
F32 = jnp.float32
BF16 = jnp.bfloat16


def shift(value, axis, step):
    devices = range(lax.axis_size(axis))
    return lax.ppermute(value, axis, [(i, i + step) for i in devices if i + step in devices])


def call(kernel, out_shape, in_specs, scratch, limit, flops, *args):
    vmem = pl.BlockSpec(memory_space=pltpu.VMEM)
    return pl.pallas_call(
        kernel,
        out_shape=out_shape,
        in_specs=in_specs,
        out_specs=tuple(vmem for _ in out_shape),
        scratch_shapes=scratch,
        compiler_params=pltpu.CompilerParams(vmem_limit_bytes=limit * 2**20),
        cost_estimate=pl.CostEstimate(flops=flops, bytes_accessed=10**6, transcendentals=0),
    )(*args)


def columns_kernel(
    tile_ref, lead_ref, tail_ref, rim_ref, held_ref, flat_ref
):
    rows, width, channels = tile_ref.shape
    held_ref[...] = tile_ref[...]
    for out_ref, first, start in ((lead_ref, 0, 0), (tail_ref, TILE - 2, width - TILE)):
        block = tile_ref[:, pl.ds(start, TILE), :].astype(F32).reshape(rows * TILE, channels)
        for h in range(channels // LANES):
            flat_ref[h] = block[:, h * LANES : (h + 1) * LANES]
        for x in range(2):
            here = pl.ds(first + x, rows, stride=TILE)
            column = [flat_ref[h, here, :] for h in range(channels // LANES)]
            out_ref[x] = jnp.concatenate(column, axis=1).astype(BF16)
    whole = width // TILE
    rim_ref[0 : 2 * whole] = tile_ref[rows - 2 : rows].reshape(2 * whole, TILE, channels)
    rim_ref[2 * whole :] = tile_ref[0:1].reshape(whole, TILE, channels)


def hold_kernel(*refs):
    count = len(refs) // 2
    for src_ref, dst_ref in zip(refs[:count], refs[count:]):
        dst_ref[...] = src_ref[...]


def down_kernel(rim_ref, left_ref, right_ref, lead_ref, tail_ref, down_ref):
    rows = left_ref.shape[1]
    parts = (left_ref, left_ref, lead_ref, tail_ref, right_ref, right_ref)
    count = down_ref.shape[0] - len(parts)
    down_ref[0:count] = rim_ref[0:count]
    for i, part in enumerate(parts):
        down_ref[count + i] = part[i % 2, rows - TILE : rows]


def up_kernel(rim_ref, left_ref, right_ref, lead_ref, tail_ref, sides_ref, up_ref):
    parts = (left_ref, left_ref, lead_ref, tail_ref, right_ref, right_ref)
    count = up_ref.shape[0] - len(parts)
    up_ref[0:count] = rim_ref[2 * count : 3 * count]
    for i, part in enumerate(parts):
        sides_ref[i] = part[i % 2]
        up_ref[count + i] = part[i % 2, 0:TILE]


def exchange(features, *small):
    rows, cols, channels = features.shape
    vmem = pl.BlockSpec(memory_space=pltpu.VMEM)
    whole = cols // TILE
    pair = jax.ShapeDtypeStruct((2, rows, channels), BF16)
    rim = jax.ShapeDtypeStruct((3 * whole, TILE, channels), BF16)
    held = jax.ShapeDtypeStruct(features.shape, BF16)
    lead, tail, rim, held = call(
        columns_kernel, (pair, pair, rim, held), [vmem],
        [pltpu.VMEM((channels // LANES, rows * TILE, LANES), F32)], 8, 10**5, features,
    )
    late, lead, tail = lax.optimization_barrier((features, lead, tail))
    below = shift(late, "row", -1)
    left = shift(tail, "col", 1)
    right = shift(lead, "col", -1)
    strips = (rim, left, right, lead, tail)
    (to_down,) = call(
        down_kernel, (jax.ShapeDtypeStruct((2 * whole + 6, TILE, channels), BF16),),
        [vmem] * 5, [], 4, 10**5, *strips,
    )
    above, small = lax.optimization_barrier((shift(to_down, "row", 1), small))
    shapes = tuple(jax.ShapeDtypeStruct(value.shape, value.dtype) for value in small)
    small = call(hold_kernel, shapes, [vmem] * len(small), [], 4, 10**5, *small)
    sides_shape = jax.ShapeDtypeStruct((6, rows, channels), BF16)
    up_shape = jax.ShapeDtypeStruct((whole + 6, TILE, channels), BF16)
    own_sides, to_up = call(
        up_kernel, (sides_shape, up_shape), [vmem] * 5, [], 4, 10**5, *strips
    )
    sides = shift(own_sides, "row", -1)
    after = shift(to_up, "row", -2)
    return below, own_sides, sides, above, after, held, small


def plan(boxes_ref, owner_ref, at_ref, by_ref, rows, cols, chips):
    row, col = lax.axis_index("row"), lax.axis_index("col")
    count = boxes_ref.shape[1]
    slot = lax.broadcasted_iota(jnp.int32, (count, LANES), 0)
    bins = lax.broadcasted_iota(jnp.int32, (count, LANES), 1).astype(F32)
    core = jnp.where(slot < chips, col % 2, 1 - col % 2)
    hop = jnp.zeros_like(slot)
    for i, step in enumerate(HOPS):
        hop = jnp.where((slot == i) | (slot == i + chips), step, hop)
    chip = col // 2 + hop * (1 - 2 * core) + chips
    chip = jnp.where(chip >= chips, chip - chips, chip)
    chip = jnp.where(chip >= chips, chip - chips, chip)
    wanted = 2 * chip + core
    fields = [jnp.zeros_like(slot) for _ in range(4)]
    for k in range(count):
        here = wanted == owner_ref[0, k]
        fields = [jnp.where(here, boxes_ref[f, k], fields[f]) for f in range(4)]
    for dim, start, size in ((0, row * rows, 2 * rows), (1, col * cols, cols)):
        lower, extent = fields[dim].astype(F32), fields[dim + 2].astype(F32)
        centre = lower + (bins + 0.5) * extent / POOL - 0.5
        centre = jnp.minimum(jnp.maximum(centre, lower), lower + extent - 1.0)
        low = jnp.floor(centre)
        for t, place in enumerate((low, low + 1.0)):
            weight = jnp.maximum(1.0 - jnp.abs(place - centre), 0.0).astype(BF16).astype(F32)
            index = place.astype(jnp.int32) - start
            inside = (index >= 0) & (index < size)
            at = jnp.minimum(jnp.maximum(index, 0), size - 1)
            at_ref[2 * dim + t] = at
            by_ref[2 * dim + t] = jnp.where(inside, weight, 0.0)
    left, right = fields[1], fields[1] + fields[3]
    hit = (left < (col + 1) * cols) & (right > col * cols)
    at_ref[4] = jnp.where(hit, 1, 0)


def spread(dst, start, value, edge_ref, sides, offset):
    count, width, channels = value.shape
    place = lax.broadcasted_iota(jnp.int32, (width, channels), 0)
    for k in range(count):
        line = value[k].astype(F32)
        low = edge_ref[sides[0], pl.ds(offset + k, 1), :]
        high = edge_ref[sides[1], pl.ds(offset + k, 1), :]
        before = jnp.where(place == 0, low, pltpu.roll(line, 1, 0))
        after = jnp.where(place == width - 1, high, pltpu.roll(line, width - 1, 0))
        dst[start + k, :, 0:channels] = before.astype(BF16)
        dst[start + k, :, channels : 2 * channels] = line.astype(BF16)
        dst[start + k, :, 2 * channels : 3 * channels] = after.astype(BF16)


def taps(src, start, count, weight, bias):
    width, depth = src.shape[1:]
    parts = [src[pl.ds(start + d, count)].reshape(count * width, depth) for d in range(3)]
    out = jnp.dot(jnp.concatenate(parts, axis=1), weight, preferred_element_type=F32)
    out = jnp.maximum(out + bias, 0.0)
    return out.reshape(count, width, out.shape[-1])


def main_kernel(
    boxes_ref, owner_ref,
    own_ref, below_ref, own_sides_ref, sides_ref, above_ref, after_ref,
    weight_hbm, bias_ref,
    tower_ref, mine_ref, other_ref,
    wide_ref, mid_ref, band_ref, comb_ref, patch_ref, strip_ref, inner_ref, weight_ref,
    at_tile, by_tile, at_ref, by_ref, sems, *, last_row, last_col,
):
    rows, width, channels = own_ref.shape
    half = mine_ref.shape[0]
    whole = width // TILE
    loads = [
        pltpu.make_async_copy(weight_hbm.at[l], weight_ref.at[l], sems.at[l]) for l in range(2)
    ]
    loads[0].start()
    plan(boxes_ref, owner_ref, at_tile, by_tile, rows, width, (last_col + 1) // 2)
    moves = [
        pltpu.make_async_copy(at_tile, at_ref, sems.at[2]),
        pltpu.make_async_copy(by_tile, by_ref, sems.at[3]),
    ]
    for move in moves:
        move.start()
    row, col = lax.axis_index("row"), lax.axis_index("col")
    for c in range(6):
        strip_ref[c, 0:2, :] = above_ref[2 * whole + c].astype(F32)[TILE - 2 : TILE]
        strip_ref[c, 2 : rows + 2, :] = own_sides_ref[c].astype(F32)
        strip_ref[c, rows + 2 : 2 * rows + 2, :] = sides_ref[c].astype(F32)
        strip_ref[c, 2 * rows + 2 : 2 * rows + 3, :] = after_ref[whole + c].astype(F32)[0:1]
        tail = strip_ref.shape[1] - (2 * rows + 3)
        strip_ref[c, 2 * rows + 3 :, :] = jnp.zeros((tail, channels), F32)
    spread(wide_ref, 0, above_ref[0 : 2 * whole].reshape(2, width, channels), strip_ref, (1, 4), 0)
    step = 8
    for part, base in ((own_ref, 2), (below_ref, 2 + rows)):
        def fill(i, carry):
            at = i * step
            spread(wide_ref, base + at, part[pl.ds(at, step)], strip_ref, (1, 4), base + at)
            return carry

        lax.fori_loop(0, rows // step, fill, 0)
    last = 2 + 2 * rows
    spread(wide_ref, last, after_ref[0:whole].reshape(1, width, channels), strip_ref, (1, 4), last)
    wide_ref[3 + 2 * rows] = jnp.zeros(wide_ref.shape[1:], BF16)

    loads[0].wait()
    loads[1].start()
    tall = inner_ref.shape[1]
    sides = []
    for side in range(2):
        parts = [
            strip_ref[3 * side + dx, dy : dy + tall, :].astype(BF16)
            for dy in range(3)
            for dx in range(3)
        ]
        sides.append(jnp.concatenate(parts, axis=1))
    out = jnp.dot(jnp.concatenate(sides, axis=0), weight_ref[0], preferred_element_type=F32)
    out = jnp.maximum(out + bias_ref[0:1], 0.0).astype(BF16).astype(F32)
    for side in range(2):
        part = out[side * tall : (side + 1) * tall]
        inner_ref[side] = jnp.where((col > 0) if side == 0 else (col < last_col), part, 0.0)

    def first(i, carry):
        at = i * FIRST
        out = taps(wide_ref, at, FIRST, weight_ref[0], bias_ref[0:1])
        spread(mid_ref, at, out.astype(BF16), inner_ref, (0, 1), at)
        return carry

    lax.fori_loop(0, (2 * rows + 2) // FIRST, first, 0)
    blank = jnp.zeros(mid_ref.shape[1:], BF16)

    @pl.when(row == 0)
    def _():
        mid_ref[0] = blank

    @pl.when(row == last_row)
    def _():
        mid_ref[rows + 1] = blank
    mid_ref[2 * rows + 1] = blank

    loads[1].wait()

    def second(i, carry):
        at = i * SECOND
        out = taps(mid_ref, at, SECOND, weight_ref[1], bias_ref[1:2])

        @pl.when(at < rows)
        def _():
            tower_ref[pl.ds(at, SECOND)] = out.astype(BF16)

        band_ref[pl.ds(at, SECOND)] = out.astype(BF16).astype(F32)
        return carry

    lax.fori_loop(0, 2 * rows // SECOND, second, 0)
    for move in moves:
        move.wait()
    halves = [(h, slice(h * LANES, (h + 1) * LANES)) for h in range(channels // LANES)]
    for side, out_ref in ((1, other_ref), (0, mine_ref)):
        def region(m, carry):
            n = m + side * half

            @pl.when(at_ref[4, n, 0] > 0)
            def _():
                for p in range(POOL):
                    line = band_ref[at_ref[0, n, p]] * by_ref[0, n, p]
                    line = line + band_ref[at_ref[1, n, p]] * by_ref[1, n, p]
                    for h, lanes in halves:
                        comb_ref[h, pl.ds(p, width, stride=SIDE), :] = line[:, lanes]
                for q in range(POOL):
                    low = pl.ds(pl.multiple_of(at_ref[2, n, q] * SIDE, SIDE), SIDE)
                    high = pl.ds(pl.multiple_of(at_ref[3, n, q] * SIDE, SIDE), SIDE)
                    for h, lanes in halves:
                        total = comb_ref[h, low, :] * by_ref[2, n, q]
                        total = total + comb_ref[h, high, :] * by_ref[3, n, q]
                        patch_ref[h, pl.ds(q, SIDE, stride=POOL), :] = total
                for h, lanes in halves:
                    out_ref[m, :, lanes] = patch_ref[h, pl.ds(0, PATCH), :].astype(BF16)

            @pl.when(at_ref[4, n, 0] == 0)
            def _():
                out_ref[m] = jnp.zeros(out_ref.shape[1:], BF16)

            return carry

        lax.fori_loop(0, half, region, 0)


def tower_and_pool(features, weight, bias, boxes, owner_slot):
    rows, cols, channels = features.shape
    below, own_sides, sides, above, after, features, small = exchange(
        features, bias, boxes.T, owner_slot
    )
    bias, boxes, owner_slot = small
    count = boxes.shape[1]
    smem = pl.BlockSpec(memory_space=pltpu.SMEM)
    vmem = pl.BlockSpec(memory_space=pltpu.VMEM)
    patches = jax.ShapeDtypeStruct((count // 2, PATCH, channels), BF16)
    kernel = functools.partial(
        main_kernel, last_row=lax.axis_size("row") - 1, last_col=lax.axis_size("col") - 1
    )
    return call(
        kernel,
        (jax.ShapeDtypeStruct(features.shape, BF16), patches, patches),
        [smem] * 2 + [vmem] * 6 + [pl.BlockSpec(memory_space=pl.ANY), vmem],
        [
            pltpu.VMEM((2 * rows + 4, cols, 3 * channels), BF16),
            pltpu.VMEM((2 * rows + 2, cols, 3 * channels), BF16),
            pltpu.VMEM((2 * rows, cols, channels), F32),
            pltpu.VMEM((channels // LANES, cols * SIDE, LANES), F32),
            pltpu.VMEM((channels // LANES, SIDE * SIDE, LANES), F32),
            pltpu.VMEM((6, 2 * rows + 24, channels), F32),
            pltpu.VMEM((2, 2 * rows + 16, channels), F32),
            pltpu.VMEM((2, 9 * channels, channels), BF16),
            pltpu.VMEM((5, count, LANES), jnp.int32),
            pltpu.VMEM((4, count, LANES), F32),
            pltpu.SMEM((5, count, LANES), jnp.int32),
            pltpu.SMEM((4, count, LANES), F32),
            pltpu.SemaphoreType.DMA((4,)),
        ],
        51, 6 * 10**9,
        boxes, owner_slot, features, below, own_sides, sides, above, after,
        weight.reshape(2, 9 * channels, channels), bias,
    )


def head_kernel(
    mine_ref, swapped_ref, ahead_ref, three_ref, two_ref,
    weight_ref, bias_ref, lift_ref, shade_ref,
    out_ref, sum_ref, wide_ref, row_ref,
):
    channels = bias_ref.shape[-1]
    halves = [(h, slice(h * LANES, (h + 1) * LANES)) for h in range(channels // LANES)]
    parts = (mine_ref[7], swapped_ref[7], ahead_ref[1], three_ref[...], two_ref[...])
    pooled = sum(part.astype(F32) for part in parts).astype(BF16).astype(F32)
    for h, lanes in halves:
        sum_ref[h, 8 : 8 + PATCH, :] = pooled[:, lanes]
    blank = jnp.zeros(wide_ref.shape[1:], BF16)
    wide_ref[0] = blank
    wide_ref[POOL + 1] = blank
    place = lax.broadcasted_iota(jnp.int32, (SIDE, LANES), 0)
    for p in range(POOL):
        for d in range(3):
            kept = (place + d - 1 >= 0) & (place + d - 1 < POOL)
            for h in range(channels // LANES):
                value = sum_ref[h, pl.ds(8 + POOL * p + d - 1, SIDE), :]
                first = d * channels + h * LANES
                wide_ref[p + 1, :, first : first + LANES] = jnp.where(kept, value, 0.0).astype(BF16)
    hidden = taps(wide_ref, 0, POOL, weight_ref[...], bias_ref[...]).astype(BF16)
    hidden = hidden.reshape(POOL * SIDE, channels)
    for u in range(2):
        lifted = []
        for v in range(2):
            value = jnp.dot(hidden, lift_ref[2 * u + v], preferred_element_type=F32)
            lifted.append(jnp.maximum(value + shade_ref[...], 0.0))
        for a in range(POOL):
            for v in range(2):
                for h, lanes in halves:
                    row_ref[a, h, pl.ds(v, SIDE, stride=2), :] = lifted[v][
                        a * SIDE : (a + 1) * SIDE, lanes
                    ]
            for h, lanes in halves:
                out_ref[0, 2 * a + u, :, lanes] = row_ref[a, h, 0 : 2 * POOL, :].astype(BF16)


def head(parts, mask_weight, mask_bias, deconv_weight, deconv_bias):
    channels = mask_bias.shape[-1]
    vmem = pl.BlockSpec(memory_space=pltpu.VMEM)
    side = 2 * POOL
    (masks,) = call(
        head_kernel,
        (jax.ShapeDtypeStruct((1, side, side, channels), BF16),),
        [vmem] * 9,
        [
            pltpu.VMEM((channels // LANES, 8 + SIDE * SIDE, LANES), F32),
            pltpu.VMEM((SIDE, SIDE, 3 * channels), BF16),
            pltpu.VMEM((POOL, channels // LANES, 2 * SIDE, LANES), F32),
        ],
        16, 10**9,
        *parts, mask_weight.reshape(9 * channels, channels), mask_bias,
        deconv_weight.reshape(4, channels, channels), deconv_bias.reshape(1, channels),
    )
    return masks


def per_device(
    features, tower_weight, tower_bias, boxes, owner_slot,
    mask_weight, mask_bias, deconv_weight, deconv_bias,
):
    peers = lax.axis_size("col")
    chips = peers // 2
    tower, mine, other = tower_and_pool(features, tower_weight, tower_bias, boxes, owner_slot)
    swapped = lax.ppermute(other, "col", [(i, i ^ 1) for i in range(peers)])

    def send(value, hop):
        steps = [2 * hop * (1 - 2 * (i % 2)) for i in range(peers)]
        return lax.ppermute(value, "col", [(i, (i + steps[i]) % peers) for i in range(peers)])

    def total(*parts):
        parts = [part.astype(F32) for part in parts]
        return sum(parts[1:], parts[0]).astype(BF16)

    ahead = send(total(mine[0:3], swapped[0:3]), 1)
    back = send(total(mine[3:5], swapped[3:5]), -1)
    two = send(total(mine[6], swapped[6], ahead[2], back[1]), -2)
    three = send(total(mine[5], swapped[5], ahead[0], back[0]), 3)
    parts = (mine, swapped, ahead, three, two)
    masks = head(parts, mask_weight, mask_bias, deconv_weight, deconv_bias)
    return tower, masks


def solution(mesh):
    placed = (P("row", "col", None), P(), P(), P("row", None), P("row", None), P(), P(), P(), P())
    return jax.shard_map(
        per_device,
        mesh=mesh,
        in_specs=placed,
        out_specs=(P("row", "col", None), P(("row", "col"), None, None, None)),
        check_vma=False,
    )
```

```python
import functools

import jax
import jax.numpy as jnp
from jax import lax
from jax.experimental import pallas as pl
from jax.experimental.pallas import tpu as pltpu
from jax.sharding import PartitionSpec as P

POOL = 14
SIDE = 16
LANES = 128
PATCH = 200
TILE = 16
FIRST = 33
SECOND = 32
HOPS = (4, 1, -1, 2, -3, 3, -2, 0)
F32 = jnp.float32
BF16 = jnp.bfloat16


def shift(value, axis, step):
    devices = range(lax.axis_size(axis))
    return lax.ppermute(value, axis, [(i, i + step) for i in devices if i + step in devices])


def call(kernel, out_shape, in_specs, scratch, limit, flops, *args):
    vmem = pl.BlockSpec(memory_space=pltpu.VMEM)
    return pl.pallas_call(
        kernel,
        out_shape=out_shape,
        in_specs=in_specs,
        out_specs=tuple(vmem for _ in out_shape),
        scratch_shapes=scratch,
        compiler_params=pltpu.CompilerParams(vmem_limit_bytes=limit * 2**20),
        cost_estimate=pl.CostEstimate(flops=flops, bytes_accessed=10**6, transcendentals=0),
    )(*args)


def columns_kernel(
    tile_ref, lead_ref, tail_ref, rim_ref, held_ref, flat_ref
):
    rows, width, channels = tile_ref.shape
    held_ref[...] = tile_ref[...]
    for out_ref, first, start in ((lead_ref, 0, 0), (tail_ref, TILE - 2, width - TILE)):
        block = tile_ref[:, pl.ds(start, TILE), :].astype(F32).reshape(rows * TILE, channels)
        for h in range(channels // LANES):
            flat_ref[h] = block[:, h * LANES : (h + 1) * LANES]
        for x in range(2):
            here = pl.ds(first + x, rows, stride=TILE)
            column = [flat_ref[h, here, :] for h in range(channels // LANES)]
            out_ref[x] = jnp.concatenate(column, axis=1).astype(BF16)
    whole = width // TILE
    rim_ref[0 : 2 * whole] = tile_ref[rows - 2 : rows].reshape(2 * whole, TILE, channels)
    rim_ref[2 * whole :] = tile_ref[0:1].reshape(whole, TILE, channels)


def hold_kernel(*refs):
    count = len(refs) // 2
    for src_ref, dst_ref in zip(refs[:count], refs[count:]):
        dst_ref[...] = src_ref[...]


def down_kernel(rim_ref, left_ref, right_ref, lead_ref, tail_ref, down_ref):
    rows = left_ref.shape[1]
    parts = (left_ref, left_ref, lead_ref, tail_ref, right_ref, right_ref)
    count = down_ref.shape[0] - len(parts)
    down_ref[0:count] = rim_ref[0:count]
    for i, part in enumerate(parts):
        down_ref[count + i] = part[i % 2, rows - TILE : rows]


def up_kernel(rim_ref, left_ref, right_ref, lead_ref, tail_ref, sides_ref, up_ref):
    parts = (left_ref, left_ref, lead_ref, tail_ref, right_ref, right_ref)
    count = up_ref.shape[0] - len(parts)
    up_ref[0:count] = rim_ref[2 * count : 3 * count]
    for i, part in enumerate(parts):
        sides_ref[i] = part[i % 2]
        up_ref[count + i] = part[i % 2, 0:TILE]


def exchange(features, *small):
    rows, cols, channels = features.shape
    vmem = pl.BlockSpec(memory_space=pltpu.VMEM)
    whole = cols // TILE
    pair = jax.ShapeDtypeStruct((2, rows, channels), BF16)
    rim = jax.ShapeDtypeStruct((3 * whole, TILE, channels), BF16)
    held = jax.ShapeDtypeStruct(features.shape, BF16)
    lead, tail, rim, held = call(
        columns_kernel, (pair, pair, rim, held), [vmem],
        [pltpu.VMEM((channels // LANES, rows * TILE, LANES), F32)], 8, 10**5, features,
    )
    late, lead, tail = lax.optimization_barrier((features, lead, tail))
    below = shift(late, "row", -1)
    left = shift(tail, "col", 1)
    right = shift(lead, "col", -1)
    strips = (rim, left, right, lead, tail)
    (to_down,) = call(
        down_kernel, (jax.ShapeDtypeStruct((2 * whole + 6, TILE, channels), BF16),),
        [vmem] * 5, [], 4, 10**5, *strips,
    )
    above, small = lax.optimization_barrier((shift(to_down, "row", 1), small))
    shapes = tuple(jax.ShapeDtypeStruct(value.shape, value.dtype) for value in small)
    small = call(hold_kernel, shapes, [vmem] * len(small), [], 4, 10**5, *small)
    sides_shape = jax.ShapeDtypeStruct((6, rows, channels), BF16)
    up_shape = jax.ShapeDtypeStruct((whole + 6, TILE, channels), BF16)
    own_sides, to_up = call(
        up_kernel, (sides_shape, up_shape), [vmem] * 5, [], 4, 10**5, *strips
    )
    sides = shift(own_sides, "row", -1)
    after = shift(to_up, "row", -2)
    return below, own_sides, sides, above, after, held, small


def plan(boxes_ref, owner_ref, at_ref, by_ref, rows, cols, chips):
    row, col = lax.axis_index("row"), lax.axis_index("col")
    count = boxes_ref.shape[1]
    slot = lax.broadcasted_iota(jnp.int32, (count, LANES), 0)
    bins = lax.broadcasted_iota(jnp.int32, (count, LANES), 1).astype(F32)
    core = jnp.where(slot < chips, col % 2, 1 - col % 2)
    hop = jnp.zeros_like(slot)
    for i, step in enumerate(HOPS):
        hop = jnp.where((slot == i) | (slot == i + chips), step, hop)
    chip = col // 2 + hop * (1 - 2 * core) + chips
    chip = jnp.where(chip >= chips, chip - chips, chip)
    chip = jnp.where(chip >= chips, chip - chips, chip)
    wanted = 2 * chip + core
    fields = [jnp.zeros_like(slot) for _ in range(4)]
    for k in range(count):
        here = wanted == owner_ref[0, k]
        fields = [jnp.where(here, boxes_ref[f, k], fields[f]) for f in range(4)]
    for dim, start, size in ((0, row * rows, 2 * rows), (1, col * cols, cols)):
        lower, extent = fields[dim].astype(F32), fields[dim + 2].astype(F32)
        centre = lower + (bins + 0.5) * extent / POOL - 0.5
        centre = jnp.minimum(jnp.maximum(centre, lower), lower + extent - 1.0)
        low = jnp.floor(centre)
        for t, place in enumerate((low, low + 1.0)):
            weight = jnp.maximum(1.0 - jnp.abs(place - centre), 0.0).astype(BF16).astype(F32)
            index = place.astype(jnp.int32) - start
            inside = (index >= 0) & (index < size)
            at = jnp.minimum(jnp.maximum(index, 0), size - 1)
            at_ref[2 * dim + t] = at
            by_ref[2 * dim + t] = jnp.where(inside, weight, 0.0)
    left, right = fields[1], fields[1] + fields[3]
    hit = (left < (col + 1) * cols) & (right > col * cols)
    at_ref[4] = jnp.where(hit, 1, 0)


def spread(dst, start, value, edge_ref, sides, offset):
    count, width, channels = value.shape
    place = lax.broadcasted_iota(jnp.int32, (width, channels), 0)
    for k in range(count):
        line = value[k].astype(F32)
        low = edge_ref[sides[0], pl.ds(offset + k, 1), :]
        high = edge_ref[sides[1], pl.ds(offset + k, 1), :]
        before = jnp.where(place == 0, low, pltpu.roll(line, 1, 0))
        after = jnp.where(place == width - 1, high, pltpu.roll(line, width - 1, 0))
        dst[start + k, :, 0:channels] = before.astype(BF16)
        dst[start + k, :, channels : 2 * channels] = line.astype(BF16)
        dst[start + k, :, 2 * channels : 3 * channels] = after.astype(BF16)


def taps(src, start, count, weight, bias):
    width, depth = src.shape[1:]
    parts = [src[pl.ds(start + d, count)].reshape(count * width, depth) for d in range(3)]
    out = jnp.dot(jnp.concatenate(parts, axis=1), weight, preferred_element_type=F32)
    out = jnp.maximum(out + bias, 0.0)
    return out.reshape(count, width, out.shape[-1])


def main_kernel(
    boxes_ref, owner_ref,
    own_ref, below_ref, own_sides_ref, sides_ref, above_ref, after_ref,
    weight_hbm, bias_ref,
    tower_ref, mine_ref, other_ref,
    wide_ref, mid_ref, band_ref, comb_ref, patch_ref, strip_ref, inner_ref, weight_ref,
    at_tile, by_tile, at_ref, by_ref, sems, *, last_row, last_col,
):
    rows, width, channels = own_ref.shape
    half = mine_ref.shape[0]
    whole = width // TILE
    loads = [
        pltpu.make_async_copy(weight_hbm.at[l], weight_ref.at[l], sems.at[l]) for l in range(2)
    ]
    loads[0].start()
    plan(boxes_ref, owner_ref, at_tile, by_tile, rows, width, (last_col + 1) // 2)
    moves = [
        pltpu.make_async_copy(at_tile, at_ref, sems.at[2]),
        pltpu.make_async_copy(by_tile, by_ref, sems.at[3]),
    ]
    for move in moves:
        move.start()
    row, col = lax.axis_index("row"), lax.axis_index("col")
    for c in range(6):
        strip_ref[c, 0:2, :] = above_ref[2 * whole + c].astype(F32)[TILE - 2 : TILE]
        strip_ref[c, 2 : rows + 2, :] = own_sides_ref[c].astype(F32)
        strip_ref[c, rows + 2 : 2 * rows + 2, :] = sides_ref[c].astype(F32)
        strip_ref[c, 2 * rows + 2 : 2 * rows + 3, :] = after_ref[whole + c].astype(F32)[0:1]
        tail = strip_ref.shape[1] - (2 * rows + 3)
        strip_ref[c, 2 * rows + 3 :, :] = jnp.zeros((tail, channels), F32)
    spread(wide_ref, 0, above_ref[0 : 2 * whole].reshape(2, width, channels), strip_ref, (1, 4), 0)
    step = 8
    for part, base in ((own_ref, 2), (below_ref, 2 + rows)):
        def fill(i, carry):
            at = i * step
            spread(wide_ref, base + at, part[pl.ds(at, step)], strip_ref, (1, 4), base + at)
            return carry

        lax.fori_loop(0, rows // step, fill, 0)
    last = 2 + 2 * rows
    spread(wide_ref, last, after_ref[0:whole].reshape(1, width, channels), strip_ref, (1, 4), last)
    wide_ref[3 + 2 * rows] = jnp.zeros(wide_ref.shape[1:], BF16)

    loads[0].wait()
    loads[1].start()
    tall = inner_ref.shape[1]
    sides = []
    for side in range(2):
        parts = [
            strip_ref[3 * side + dx, dy : dy + tall, :].astype(BF16)
            for dy in range(3)
            for dx in range(3)
        ]
        sides.append(jnp.concatenate(parts, axis=1))
    out = jnp.dot(jnp.concatenate(sides, axis=0), weight_ref[0], preferred_element_type=F32)
    out = jnp.maximum(out + bias_ref[0:1], 0.0).astype(BF16).astype(F32)
    for side in range(2):
        part = out[side * tall : (side + 1) * tall]
        inner_ref[side] = jnp.where((col > 0) if side == 0 else (col < last_col), part, 0.0)

    def first(i, carry):
        at = i * FIRST
        out = taps(wide_ref, at, FIRST, weight_ref[0], bias_ref[0:1])
        spread(mid_ref, at, out.astype(BF16), inner_ref, (0, 1), at)
        return carry

    lax.fori_loop(0, (2 * rows + 2) // FIRST, first, 0)
    blank = jnp.zeros(mid_ref.shape[1:], BF16)

    @pl.when(row == 0)
    def _():
        mid_ref[0] = blank

    @pl.when(row == last_row)
    def _():
        mid_ref[rows + 1] = blank
    mid_ref[2 * rows + 1] = blank

    loads[1].wait()

    def second(i, carry):
        at = i * SECOND
        out = taps(mid_ref, at, SECOND, weight_ref[1], bias_ref[1:2])

        @pl.when(at < rows)
        def _():
            tower_ref[pl.ds(at, SECOND)] = out.astype(BF16)

        band_ref[pl.ds(at, SECOND)] = out.astype(BF16).astype(F32)
        return carry

    lax.fori_loop(0, 2 * rows // SECOND, second, 0)
    for move in moves:
        move.wait()
    halves = [(h, slice(h * LANES, (h + 1) * LANES)) for h in range(channels // LANES)]
    for side, out_ref in ((1, other_ref), (0, mine_ref)):
        def region(m, carry):
            n = m + side * half

            @pl.when(at_ref[4, n, 0] > 0)
            def _():
                for p in range(POOL):
                    line = band_ref[at_ref[0, n, p]] * by_ref[0, n, p]
                    line = line + band_ref[at_ref[1, n, p]] * by_ref[1, n, p]
                    for h, lanes in halves:
                        comb_ref[h, pl.ds(p, width, stride=SIDE), :] = line[:, lanes]
                for q in range(POOL):
                    low = pl.ds(pl.multiple_of(at_ref[2, n, q] * SIDE, SIDE), SIDE)
                    high = pl.ds(pl.multiple_of(at_ref[3, n, q] * SIDE, SIDE), SIDE)
                    for h, lanes in halves:
                        total = comb_ref[h, low, :] * by_ref[2, n, q]
                        total = total + comb_ref[h, high, :] * by_ref[3, n, q]
                        patch_ref[h, pl.ds(q, SIDE, stride=POOL), :] = total
                for h, lanes in halves:
                    out_ref[m, :, lanes] = patch_ref[h, pl.ds(0, PATCH), :].astype(BF16)

            @pl.when(at_ref[4, n, 0] == 0)
            def _():
                out_ref[m] = jnp.zeros(out_ref.shape[1:], BF16)

            return carry

        lax.fori_loop(0, half, region, 0)


def tower_and_pool(features, weight, bias, boxes, owner_slot):
    rows, cols, channels = features.shape
    below, own_sides, sides, above, after, features, small = exchange(
        features, bias, boxes.T, owner_slot
    )
    bias, boxes, owner_slot = small
    count = boxes.shape[1]
    smem = pl.BlockSpec(memory_space=pltpu.SMEM)
    vmem = pl.BlockSpec(memory_space=pltpu.VMEM)
    patches = jax.ShapeDtypeStruct((count // 2, PATCH, channels), BF16)
    kernel = functools.partial(
        main_kernel, last_row=lax.axis_size("row") - 1, last_col=lax.axis_size("col") - 1
    )
    return call(
        kernel,
        (jax.ShapeDtypeStruct(features.shape, BF16), patches, patches),
        [smem] * 2 + [vmem] * 6 + [pl.BlockSpec(memory_space=pl.ANY), vmem],
        [
            pltpu.VMEM((2 * rows + 4, cols, 3 * channels), BF16),
            pltpu.VMEM((2 * rows + 2, cols, 3 * channels), BF16),
            pltpu.VMEM((2 * rows, cols, channels), F32),
            pltpu.VMEM((channels // LANES, cols * SIDE, LANES), F32),
            pltpu.VMEM((channels // LANES, SIDE * SIDE, LANES), F32),
            pltpu.VMEM((6, 2 * rows + 24, channels), F32),
            pltpu.VMEM((2, 2 * rows + 16, channels), F32),
            pltpu.VMEM((2, 9 * channels, channels), BF16),
            pltpu.VMEM((5, count, LANES), jnp.int32),
            pltpu.VMEM((4, count, LANES), F32),
            pltpu.SMEM((5, count, LANES), jnp.int32),
            pltpu.SMEM((4, count, LANES), F32),
            pltpu.SemaphoreType.DMA((4,)),
        ],
        51, 6 * 10**9,
        boxes, owner_slot, features, below, own_sides, sides, above, after,
        weight.reshape(2, 9 * channels, channels), bias,
    )


def head_kernel(
    mine_ref, swapped_ref, ahead_ref, two_ref, three_ref,
    weight_ref, bias_ref, lift_ref, shade_ref,
    out_ref, sum_ref, wide_ref, row_ref,
):
    channels = bias_ref.shape[-1]
    halves = [(h, slice(h * LANES, (h + 1) * LANES)) for h in range(channels // LANES)]
    parts = (mine_ref[7], swapped_ref[7], ahead_ref[1], three_ref[...], two_ref[...])
    pooled = sum(part.astype(F32) for part in parts).astype(BF16).astype(F32)
    for h, lanes in halves:
        sum_ref[h, 8 : 8 + PATCH, :] = pooled[:, lanes]
    blank = jnp.zeros(wide_ref.shape[1:], BF16)
    wide_ref[0] = blank
    wide_ref[POOL + 1] = blank
    place = lax.broadcasted_iota(jnp.int32, (SIDE, LANES), 0)
    for p in range(POOL):
        for d in range(3):
            kept = (place + d - 1 >= 0) & (place + d - 1 < POOL)
            for h in range(channels // LANES):
                value = sum_ref[h, pl.ds(8 + POOL * p + d - 1, SIDE), :]
                first = d * channels + h * LANES
                wide_ref[p + 1, :, first : first + LANES] = jnp.where(kept, value, 0.0).astype(BF16)
    hidden = taps(wide_ref, 0, POOL, weight_ref[...], bias_ref[...]).astype(BF16)
    hidden = hidden.reshape(POOL * SIDE, channels)
    for u in range(2):
        lifted = []
        for v in range(2):
            value = jnp.dot(hidden, lift_ref[2 * u + v], preferred_element_type=F32)
            lifted.append(jnp.maximum(value + shade_ref[...], 0.0))
        for a in range(POOL):
            for v in range(2):
                for h, lanes in halves:
                    row_ref[a, h, pl.ds(v, SIDE, stride=2), :] = lifted[v][
                        a * SIDE : (a + 1) * SIDE, lanes
                    ]
            for h, lanes in halves:
                out_ref[0, 2 * a + u, :, lanes] = row_ref[a, h, 0 : 2 * POOL, :].astype(BF16)


def head(parts, mask_weight, mask_bias, deconv_weight, deconv_bias):
    channels = mask_bias.shape[-1]
    vmem = pl.BlockSpec(memory_space=pltpu.VMEM)
    side = 2 * POOL
    (masks,) = call(
        head_kernel,
        (jax.ShapeDtypeStruct((1, side, side, channels), BF16),),
        [vmem] * 9,
        [
            pltpu.VMEM((channels // LANES, 8 + SIDE * SIDE, LANES), F32),
            pltpu.VMEM((SIDE, SIDE, 3 * channels), BF16),
            pltpu.VMEM((POOL, channels // LANES, 2 * SIDE, LANES), F32),
        ],
        16, 10**9,
        *parts, mask_weight.reshape(9 * channels, channels), mask_bias,
        deconv_weight.reshape(4, channels, channels), deconv_bias.reshape(1, channels),
    )
    return masks


def per_device(
    features, tower_weight, tower_bias, boxes, owner_slot,
    mask_weight, mask_bias, deconv_weight, deconv_bias,
):
    peers = lax.axis_size("col")
    chips = peers // 2
    tower, mine, other = tower_and_pool(features, tower_weight, tower_bias, boxes, owner_slot)
    swapped = lax.ppermute(other, "col", [(i, i ^ 1) for i in range(peers)])

    def send(value, hop):
        steps = [2 * hop * (1 - 2 * (i % 2)) for i in range(peers)]
        return lax.ppermute(value, "col", [(i, (i + steps[i]) % peers) for i in range(peers)])

    def total(*parts):
        parts = [part.astype(F32) for part in parts]
        return sum(parts[1:], parts[0]).astype(BF16)

    ahead = send(total(mine[0:3], swapped[0:3]), 1)
    back = send(total(mine[3:5], swapped[3:5]), -1)
    two = send(total(mine[6], swapped[6], ahead[2], back[1]), -2)
    three = send(total(mine[5], swapped[5], ahead[0], back[0]), 3)
    parts = (mine, swapped, ahead, two, three)
    masks = head(parts, mask_weight, mask_bias, deconv_weight, deconv_bias)
    return tower, masks


def solution(mesh):
    placed = (P("row", "col", None), P(), P(), P("row", None), P("row", None), P(), P(), P(), P())
    return jax.shard_map(
        per_device,
        mesh=mesh,
        in_specs=placed,
        out_specs=(P("row", "col", None), P(("row", "col"), None, None, None)),
        check_vma=False,
    )
```

```python
import functools

import jax
import jax.numpy as jnp
from jax import lax
from jax.experimental import pallas as pl
from jax.experimental.pallas import tpu as pltpu
from jax.sharding import PartitionSpec as P

POOL = 14
SIDE = 16
LANES = 128
PATCH = 200
TILE = 16
FIRST = 33
SECOND = 32
HOPS = (4, 1, -1, 2, -3, 3, -2, 0)
F32 = jnp.float32
BF16 = jnp.bfloat16


def shift(value, axis, step):
    devices = range(lax.axis_size(axis))
    return lax.ppermute(value, axis, [(i, i + step) for i in devices if i + step in devices])


def call(kernel, out_shape, in_specs, scratch, limit, flops, *args):
    vmem = pl.BlockSpec(memory_space=pltpu.VMEM)
    return pl.pallas_call(
        kernel,
        out_shape=out_shape,
        in_specs=in_specs,
        out_specs=tuple(vmem for _ in out_shape),
        scratch_shapes=scratch,
        compiler_params=pltpu.CompilerParams(vmem_limit_bytes=limit * 2**20),
        cost_estimate=pl.CostEstimate(flops=flops, bytes_accessed=10**6, transcendentals=0),
    )(*args)


def columns_kernel(
    tile_ref, lead_ref, tail_ref, rim_ref, held_ref, flat_ref
):
    rows, width, channels = tile_ref.shape
    held_ref[...] = tile_ref[...]
    for out_ref, first, start in ((lead_ref, 0, 0), (tail_ref, TILE - 2, width - TILE)):
        block = tile_ref[:, pl.ds(start, TILE), :].astype(F32).reshape(rows * TILE, channels)
        for h in range(channels // LANES):
            flat_ref[h] = block[:, h * LANES : (h + 1) * LANES]
        for x in range(2):
            here = pl.ds(first + x, rows, stride=TILE)
            column = [flat_ref[h, here, :] for h in range(channels // LANES)]
            out_ref[x] = jnp.concatenate(column, axis=1).astype(BF16)
    whole = width // TILE
    rim_ref[0 : 2 * whole] = tile_ref[rows - 2 : rows].reshape(2 * whole, TILE, channels)
    rim_ref[2 * whole :] = tile_ref[0:1].reshape(whole, TILE, channels)


def hold_kernel(*refs):
    count = len(refs) // 2
    for src_ref, dst_ref in zip(refs[:count], refs[count:]):
        dst_ref[...] = src_ref[...]


def down_kernel(rim_ref, left_ref, right_ref, lead_ref, tail_ref, down_ref):
    rows = left_ref.shape[1]
    parts = (left_ref, left_ref, lead_ref, tail_ref, right_ref, right_ref)
    count = down_ref.shape[0] - len(parts)
    down_ref[0:count] = rim_ref[0:count]
    for i, part in enumerate(parts):
        down_ref[count + i] = part[i % 2, rows - TILE : rows]


def up_kernel(rim_ref, left_ref, right_ref, lead_ref, tail_ref, sides_ref, up_ref):
    parts = (left_ref, left_ref, lead_ref, tail_ref, right_ref, right_ref)
    count = up_ref.shape[0] - len(parts)
    up_ref[0:count] = rim_ref[2 * count : 3 * count]
    for i, part in enumerate(parts):
        sides_ref[i] = part[i % 2]
        up_ref[count + i] = part[i % 2, 0:TILE]


def exchange(features, *small):
    rows, cols, channels = features.shape
    vmem = pl.BlockSpec(memory_space=pltpu.VMEM)
    whole = cols // TILE
    pair = jax.ShapeDtypeStruct((2, rows, channels), BF16)
    rim = jax.ShapeDtypeStruct((3 * whole, TILE, channels), BF16)
    held = jax.ShapeDtypeStruct(features.shape, BF16)
    lead, tail, rim, held = call(
        columns_kernel, (pair, pair, rim, held), [vmem],
        [pltpu.VMEM((channels // LANES, rows * TILE, LANES), F32)], 8, 10**5, features,
    )
    late, lead, tail = lax.optimization_barrier((features, lead, tail))
    below = shift(late, "row", -1)
    left = shift(tail, "col", 1)
    right = shift(lead, "col", -1)
    strips = (rim, left, right, lead, tail)
    (to_down,) = call(
        down_kernel, (jax.ShapeDtypeStruct((2 * whole + 6, TILE, channels), BF16),),
        [vmem] * 5, [], 4, 10**5, *strips,
    )
    above = shift(to_down, "row", 1)
    sides_shape = jax.ShapeDtypeStruct((6, rows, channels), BF16)
    up_shape = jax.ShapeDtypeStruct((whole + 6, TILE, channels), BF16)
    own_sides, to_up = call(
        up_kernel, (sides_shape, up_shape), [vmem] * 5, [], 4, 10**5, *strips
    )
    sides = shift(own_sides, "row", -1)
    after = shift(to_up, "row", -2)
    small, _ = lax.optimization_barrier((small, (to_down, to_up)))
    shapes = tuple(jax.ShapeDtypeStruct(value.shape, value.dtype) for value in small)
    small = call(hold_kernel, shapes, [vmem] * len(small), [], 4, 10**5, *small)
    return below, own_sides, sides, above, after, held, small


def plan(boxes_ref, owner_ref, at_ref, by_ref, rows, cols, chips):
    row, col = lax.axis_index("row"), lax.axis_index("col")
    count = boxes_ref.shape[1]
    slot = lax.broadcasted_iota(jnp.int32, (count, LANES), 0)
    bins = lax.broadcasted_iota(jnp.int32, (count, LANES), 1).astype(F32)
    core = jnp.where(slot < chips, col % 2, 1 - col % 2)
    hop = jnp.zeros_like(slot)
    for i, step in enumerate(HOPS):
        hop = jnp.where((slot == i) | (slot == i + chips), step, hop)
    chip = col // 2 + hop * (1 - 2 * core) + chips
    chip = jnp.where(chip >= chips, chip - chips, chip)
    chip = jnp.where(chip >= chips, chip - chips, chip)
    wanted = 2 * chip + core
    fields = [jnp.zeros_like(slot) for _ in range(4)]
    for k in range(count):
        here = wanted == owner_ref[0, k]
        fields = [jnp.where(here, boxes_ref[f, k], fields[f]) for f in range(4)]
    for dim, start, size in ((0, row * rows, 2 * rows), (1, col * cols, cols)):
        lower, extent = fields[dim].astype(F32), fields[dim + 2].astype(F32)
        centre = lower + (bins + 0.5) * extent / POOL - 0.5
        centre = jnp.minimum(jnp.maximum(centre, lower), lower + extent - 1.0)
        low = jnp.floor(centre)
        for t, place in enumerate((low, low + 1.0)):
            weight = jnp.maximum(1.0 - jnp.abs(place - centre), 0.0).astype(BF16).astype(F32)
            index = place.astype(jnp.int32) - start
            inside = (index >= 0) & (index < size)
            at = jnp.minimum(jnp.maximum(index, 0), size - 1)
            at_ref[2 * dim + t] = at
            by_ref[2 * dim + t] = jnp.where(inside, weight, 0.0)
    left, right = fields[1], fields[1] + fields[3]
    hit = (left < (col + 1) * cols) & (right > col * cols)
    at_ref[4] = jnp.where(hit, 1, 0)


def spread(dst, start, value, edge_ref, sides, offset):
    count, width, channels = value.shape
    place = lax.broadcasted_iota(jnp.int32, (width, channels), 0)
    for k in range(count):
        line = value[k].astype(F32)
        low = edge_ref[sides[0], pl.ds(offset + k, 1), :]
        high = edge_ref[sides[1], pl.ds(offset + k, 1), :]
        before = jnp.where(place == 0, low, pltpu.roll(line, 1, 0))
        after = jnp.where(place == width - 1, high, pltpu.roll(line, width - 1, 0))
        dst[start + k, :, 0:channels] = before.astype(BF16)
        dst[start + k, :, channels : 2 * channels] = line.astype(BF16)
        dst[start + k, :, 2 * channels : 3 * channels] = after.astype(BF16)


def taps(src, start, count, weight, bias):
    width, depth = src.shape[1:]
    parts = [src[pl.ds(start + d, count)].reshape(count * width, depth) for d in range(3)]
    out = jnp.dot(jnp.concatenate(parts, axis=1), weight, preferred_element_type=F32)
    out = jnp.maximum(out + bias, 0.0)
    return out.reshape(count, width, out.shape[-1])


def main_kernel(
    boxes_ref, owner_ref,
    own_ref, below_ref, own_sides_ref, sides_ref, above_ref, after_ref,
    weight_hbm, bias_ref,
    tower_ref, mine_ref, other_ref,
    wide_ref, mid_ref, band_ref, comb_ref, patch_ref, strip_ref, inner_ref, weight_ref,
    at_tile, by_tile, at_ref, by_ref, sems, *, last_row, last_col,
):
    rows, width, channels = own_ref.shape
    half = mine_ref.shape[0]
    whole = width // TILE
    loads = [
        pltpu.make_async_copy(weight_hbm.at[l], weight_ref.at[l], sems.at[l]) for l in range(2)
    ]
    loads[0].start()
    plan(boxes_ref, owner_ref, at_tile, by_tile, rows, width, (last_col + 1) // 2)
    moves = [
        pltpu.make_async_copy(at_tile, at_ref, sems.at[2]),
        pltpu.make_async_copy(by_tile, by_ref, sems.at[3]),
    ]
    for move in moves:
        move.start()
    row, col = lax.axis_index("row"), lax.axis_index("col")
    for c in range(6):
        strip_ref[c, 0:2, :] = above_ref[2 * whole + c].astype(F32)[TILE - 2 : TILE]
        strip_ref[c, 2 : rows + 2, :] = own_sides_ref[c].astype(F32)
        strip_ref[c, rows + 2 : 2 * rows + 2, :] = sides_ref[c].astype(F32)
        strip_ref[c, 2 * rows + 2 : 2 * rows + 3, :] = after_ref[whole + c].astype(F32)[0:1]
        tail = strip_ref.shape[1] - (2 * rows + 3)
        strip_ref[c, 2 * rows + 3 :, :] = jnp.zeros((tail, channels), F32)
    spread(wide_ref, 0, above_ref[0 : 2 * whole].reshape(2, width, channels), strip_ref, (1, 4), 0)
    step = 8
    for part, base in ((own_ref, 2), (below_ref, 2 + rows)):
        def fill(i, carry):
            at = i * step
            spread(wide_ref, base + at, part[pl.ds(at, step)], strip_ref, (1, 4), base + at)
            return carry

        lax.fori_loop(0, rows // step, fill, 0)
    last = 2 + 2 * rows
    spread(wide_ref, last, after_ref[0:whole].reshape(1, width, channels), strip_ref, (1, 4), last)
    wide_ref[3 + 2 * rows] = jnp.zeros(wide_ref.shape[1:], BF16)

    loads[0].wait()
    loads[1].start()
    tall = inner_ref.shape[1]
    sides = []
    for side in range(2):
        parts = [
            strip_ref[3 * side + dx, dy : dy + tall, :].astype(BF16)
            for dy in range(3)
            for dx in range(3)
        ]
        sides.append(jnp.concatenate(parts, axis=1))
    out = jnp.dot(jnp.concatenate(sides, axis=0), weight_ref[0], preferred_element_type=F32)
    out = jnp.maximum(out + bias_ref[0:1], 0.0).astype(BF16).astype(F32)
    for side in range(2):
        part = out[side * tall : (side + 1) * tall]
        inner_ref[side] = jnp.where((col > 0) if side == 0 else (col < last_col), part, 0.0)

    def first(i, carry):
        at = i * FIRST
        out = taps(wide_ref, at, FIRST, weight_ref[0], bias_ref[0:1])
        spread(mid_ref, at, out.astype(BF16), inner_ref, (0, 1), at)
        return carry

    lax.fori_loop(0, (2 * rows + 2) // FIRST, first, 0)
    blank = jnp.zeros(mid_ref.shape[1:], BF16)

    @pl.when(row == 0)
    def _():
        mid_ref[0] = blank

    @pl.when(row == last_row)
    def _():
        mid_ref[rows + 1] = blank
    mid_ref[2 * rows + 1] = blank

    loads[1].wait()

    def second(i, carry):
        at = i * SECOND
        out = taps(mid_ref, at, SECOND, weight_ref[1], bias_ref[1:2])

        @pl.when(at < rows)
        def _():
            tower_ref[pl.ds(at, SECOND)] = out.astype(BF16)

        band_ref[pl.ds(at, SECOND)] = out.astype(BF16).astype(F32)
        return carry

    lax.fori_loop(0, 2 * rows // SECOND, second, 0)
    for move in moves:
        move.wait()
    halves = [(h, slice(h * LANES, (h + 1) * LANES)) for h in range(channels // LANES)]
    for side, out_ref in ((1, other_ref), (0, mine_ref)):
        def region(m, carry):
            n = m + side * half

            @pl.when(at_ref[4, n, 0] > 0)
            def _():
                for p in range(POOL):
                    line = band_ref[at_ref[0, n, p]] * by_ref[0, n, p]
                    line = line + band_ref[at_ref[1, n, p]] * by_ref[1, n, p]
                    for h, lanes in halves:
                        comb_ref[h, pl.ds(p, width, stride=SIDE), :] = line[:, lanes]
                for q in range(POOL):
                    low = pl.ds(pl.multiple_of(at_ref[2, n, q] * SIDE, SIDE), SIDE)
                    high = pl.ds(pl.multiple_of(at_ref[3, n, q] * SIDE, SIDE), SIDE)
                    for h, lanes in halves:
                        total = comb_ref[h, low, :] * by_ref[2, n, q]
                        total = total + comb_ref[h, high, :] * by_ref[3, n, q]
                        patch_ref[h, pl.ds(q, SIDE, stride=POOL), :] = total
                for h, lanes in halves:
                    out_ref[m, :, lanes] = patch_ref[h, pl.ds(0, PATCH), :].astype(BF16)

            @pl.when(at_ref[4, n, 0] == 0)
            def _():
                out_ref[m] = jnp.zeros(out_ref.shape[1:], BF16)

            return carry

        lax.fori_loop(0, half, region, 0)


def tower_and_pool(features, weight, bias, boxes, owner_slot):
    rows, cols, channels = features.shape
    below, own_sides, sides, above, after, features, small = exchange(
        features, bias, boxes.T, owner_slot
    )
    bias, boxes, owner_slot = small
    count = boxes.shape[1]
    smem = pl.BlockSpec(memory_space=pltpu.SMEM)
    vmem = pl.BlockSpec(memory_space=pltpu.VMEM)
    patches = jax.ShapeDtypeStruct((count // 2, PATCH, channels), BF16)
    kernel = functools.partial(
        main_kernel, last_row=lax.axis_size("row") - 1, last_col=lax.axis_size("col") - 1
    )
    return call(
        kernel,
        (jax.ShapeDtypeStruct(features.shape, BF16), patches, patches),
        [smem] * 2 + [vmem] * 6 + [pl.BlockSpec(memory_space=pl.ANY), vmem],
        [
            pltpu.VMEM((2 * rows + 4, cols, 3 * channels), BF16),
            pltpu.VMEM((2 * rows + 2, cols, 3 * channels), BF16),
            pltpu.VMEM((2 * rows, cols, channels), F32),
            pltpu.VMEM((channels // LANES, cols * SIDE, LANES), F32),
            pltpu.VMEM((channels // LANES, SIDE * SIDE, LANES), F32),
            pltpu.VMEM((6, 2 * rows + 24, channels), F32),
            pltpu.VMEM((2, 2 * rows + 16, channels), F32),
            pltpu.VMEM((2, 9 * channels, channels), BF16),
            pltpu.VMEM((5, count, LANES), jnp.int32),
            pltpu.VMEM((4, count, LANES), F32),
            pltpu.SMEM((5, count, LANES), jnp.int32),
            pltpu.SMEM((4, count, LANES), F32),
            pltpu.SemaphoreType.DMA((4,)),
        ],
        51, 6 * 10**9,
        boxes, owner_slot, features, below, own_sides, sides, above, after,
        weight.reshape(2, 9 * channels, channels), bias,
    )


def head_kernel(
    mine_ref, swapped_ref, ahead_ref, two_ref, three_ref,
    weight_ref, bias_ref, lift_ref, shade_ref,
    out_ref, sum_ref, wide_ref, row_ref,
):
    channels = bias_ref.shape[-1]
    halves = [(h, slice(h * LANES, (h + 1) * LANES)) for h in range(channels // LANES)]
    parts = (mine_ref[7], swapped_ref[7], ahead_ref[1], three_ref[...], two_ref[...])
    pooled = sum(part.astype(F32) for part in parts).astype(BF16).astype(F32)
    for h, lanes in halves:
        sum_ref[h, 8 : 8 + PATCH, :] = pooled[:, lanes]
    blank = jnp.zeros(wide_ref.shape[1:], BF16)
    wide_ref[0] = blank
    wide_ref[POOL + 1] = blank
    place = lax.broadcasted_iota(jnp.int32, (SIDE, LANES), 0)
    for p in range(POOL):
        for d in range(3):
            kept = (place + d - 1 >= 0) & (place + d - 1 < POOL)
            for h in range(channels // LANES):
                value = sum_ref[h, pl.ds(8 + POOL * p + d - 1, SIDE), :]
                first = d * channels + h * LANES
                wide_ref[p + 1, :, first : first + LANES] = jnp.where(kept, value, 0.0).astype(BF16)
    hidden = taps(wide_ref, 0, POOL, weight_ref[...], bias_ref[...]).astype(BF16)
    hidden = hidden.reshape(POOL * SIDE, channels)
    for u in range(2):
        lifted = []
        for v in range(2):
            value = jnp.dot(hidden, lift_ref[2 * u + v], preferred_element_type=F32)
            lifted.append(jnp.maximum(value + shade_ref[...], 0.0))
        for a in range(POOL):
            for v in range(2):
                for h, lanes in halves:
                    row_ref[a, h, pl.ds(v, SIDE, stride=2), :] = lifted[v][
                        a * SIDE : (a + 1) * SIDE, lanes
                    ]
            for h, lanes in halves:
                out_ref[0, 2 * a + u, :, lanes] = row_ref[a, h, 0 : 2 * POOL, :].astype(BF16)


def head(parts, mask_weight, mask_bias, deconv_weight, deconv_bias):
    channels = mask_bias.shape[-1]
    vmem = pl.BlockSpec(memory_space=pltpu.VMEM)
    side = 2 * POOL
    (masks,) = call(
        head_kernel,
        (jax.ShapeDtypeStruct((1, side, side, channels), BF16),),
        [vmem] * 9,
        [
            pltpu.VMEM((channels // LANES, 8 + SIDE * SIDE, LANES), F32),
            pltpu.VMEM((SIDE, SIDE, 3 * channels), BF16),
            pltpu.VMEM((POOL, channels // LANES, 2 * SIDE, LANES), F32),
        ],
        16, 10**9,
        *parts, mask_weight.reshape(9 * channels, channels), mask_bias,
        deconv_weight.reshape(4, channels, channels), deconv_bias.reshape(1, channels),
    )
    return masks


def per_device(
    features, tower_weight, tower_bias, boxes, owner_slot,
    mask_weight, mask_bias, deconv_weight, deconv_bias,
):
    peers = lax.axis_size("col")
    chips = peers // 2
    tower, mine, other = tower_and_pool(features, tower_weight, tower_bias, boxes, owner_slot)
    swapped = lax.ppermute(other, "col", [(i, i ^ 1) for i in range(peers)])

    def send(value, hop):
        steps = [2 * hop * (1 - 2 * (i % 2)) for i in range(peers)]
        return lax.ppermute(value, "col", [(i, (i + steps[i]) % peers) for i in range(peers)])

    def total(*parts):
        parts = [part.astype(F32) for part in parts]
        return sum(parts[1:], parts[0]).astype(BF16)

    ahead = send(total(mine[0:3], swapped[0:3]), 1)
    back = send(total(mine[3:5], swapped[3:5]), -1)
    two = send(total(mine[6], swapped[6], ahead[2], back[1]), -2)
    three = send(total(mine[5], swapped[5], ahead[0], back[0]), 3)
    parts = (mine, swapped, ahead, two, three)
    masks = head(parts, mask_weight, mask_bias, deconv_weight, deconv_bias)
    return tower, masks


def solution(mesh):
    placed = (P("row", "col", None), P(), P(), P("row", None), P("row", None), P(), P(), P(), P())
    return jax.shard_map(
        per_device,
        mesh=mesh,
        in_specs=placed,
        out_specs=(P("row", "col", None), P(("row", "col"), None, None, None)),
        check_vma=False,
    )
```
